128 devices in a mesh: ctx: 32 (over z, y, core), exp: 4 (over x).
Axes of the slice: x: 4, y: 4, z: 4, core: 2. Of those that a mesh axis runs over, the one named last changes fastest.
Arguments:
- tokens: bfloat16 [4096, 4096], P('ctx'), may hold values from -6 to 6
- ada_shift: float32 [4096], replicated, may hold values from -3 to 3
- ada_scale: float32 [4096], replicated, may hold values from -3 to 3
- ada_gate: float32 [4096], replicated, may hold values from -6 to 6
- router: bfloat16 [4, 4096, 2], P('exp'), may hold values from -0.09375 to 0.09375
- expert_up: bfloat16 [4, 4096, 16384], P('exp', None, 'ctx'), may hold values from -0.09375 to 0.09375
- expert_down: bfloat16 [4, 16384, 4096], P('exp', 'ctx'), may hold values from -0.0625 to 0.0625
- picked_ids: int32 [4, 2, 128], P('exp'), may hold values from 0 to 4095, as said below
- out_grad: bfloat16 [4096, 4096], P('ctx'), may hold values from -6 to 6
Outputs:
- block_out: bfloat16 [4096, 4096], P('ctx')
- tokens_grad: bfloat16 [4096, 4096], P('ctx')
- up_grad: bfloat16 [4, 4096, 16384], P('exp', None, 'ctx')
- down_grad: bfloat16 [4, 16384, 4096], P('exp', 'ctx')
- router_grad: float32 [4, 4096, 2], P('exp')
- shift_grad: float32 [4096], replicated
- scale_grad: float32 [4096], replicated
- gate_grad: float32 [4096], replicated
The draws below stay inside these ranges and needn't reach their ends.
Inputs may be any that keep to these rules, and one draw needn't show every extreme that they name: Row picked_ids[e, j] lists 128 distinct tokens for expert e * 2 + j. Among the 128 tokens of any one index of ctx it picks at most 8, and for each expert exactly 8 from at least one such index.
All inputs are finite; a program needn't handle non-finite values.
Results may differ from the reference program's by a relative error of at most 0.007.
Values may be sent and summed in bfloat16 or wider, within the bound.
A program may use at most 128 MiB of HBM per device.

```python
import jax
import jax.numpy as jnp
from jax import lax

D = 4096
HID = 8192
PAIR = 2
TOK_DEV = 128
MOST = 8
TOKENS = 4096
CAP = 128
N_CTX = 32
N_EXP = 4


def draw_picked_ids(key, part):
    slot_total = N_CTX * MOST

    def one_expert(expert_key):
        key_full, key_rank, key_tok = jax.random.split(expert_key, 3)
        full_shard = jax.random.randint(key_full, (), 0, N_CTX)
        ranking = jax.random.permutation(key_rank, slot_total).astype(jnp.int32)
        shard_of = jnp.arange(slot_total, dtype=jnp.int32) // MOST
        within = jnp.arange(slot_total, dtype=jnp.int32) % MOST
        scores = jnp.where(shard_of == full_shard, -1, ranking)
        chosen_slots = jnp.argsort(scores, stable=True)[:CAP]
        shard_keys = jax.random.split(key_tok, N_CTX)
        shuffles = jax.vmap(lambda each_key: jax.random.permutation(each_key, TOK_DEV))(shard_keys).astype(jnp.int32)
        token_ids = shard_of * TOK_DEV + shuffles[shard_of, within]
        return token_ids[chosen_slots].astype(jnp.int32)
    expert_keys = jax.random.split(jax.random.fold_in(key, 7), N_EXP * PAIR)
    return jax.vmap(one_expert)(expert_keys).reshape(N_EXP, PAIR, CAP)


def shard_levels(rng, extent, cuts, smallest, largest):
    gain = 1.0
    for position, blocks in cuts:
        heights = jax.random.uniform(jax.random.fold_in(jax.random.fold_in(rng, 6), position), (blocks,), jnp.float32, smallest / len(cuts), largest / len(cuts))
        gain = gain * jnp.repeat(jnp.exp(heights), extent[position] // blocks).reshape((-1,) + (1,) * (len(extent) - 1 - position))
    return gain


def scatter_about(key, shape, scale, most, cuts=(), kind=jnp.bfloat16):
    drawn = jax.random.normal(key, shape, jnp.float32) * scale
    if len(cuts) > 0:
        drawn = shard_levels(key, shape, cuts, -0.22, 0.18) * drawn
    return jnp.clip(drawn, min=-most, max=most).astype(kind)


def setup_inputs(seed: int = 0) -> dict:
    splits = jax.random.split(jax.random.key(seed), 10)
    tokens = scatter_about(splits[0], (TOKENS, D), 1.0, 6.0, ((0, 32),))
    ada_shift = scatter_about(splits[1], (D,), 0.5, 3.0, (), jnp.float32)
    ada_scale = scatter_about(splits[2], (D,), 0.5, 3.0, (), jnp.float32)
    ada_gate = scatter_about(splits[3], (D,), 1.5, 6.0, (), jnp.float32)
    router = scatter_about(splits[4], (N_EXP, D, PAIR), D ** -0.5, 0.09375, ((0, 4),))
    expert_up = scatter_about(splits[5], (N_EXP, D, PAIR * HID), D ** -0.5, 0.09375, ((0, 4), (2, 32)))
    expert_down = scatter_about(splits[6], (N_EXP, PAIR * HID, D), HID ** -0.5, 0.0625, ((0, 4), (1, 32)))
    picked_ids = draw_picked_ids(jax.random.fold_in(splits[9], 71), 0)
    out_grad = scatter_about(splits[8], (TOKENS, D), 1.0, 6.0, ((0, 32),))
    return dict(tokens=tokens, ada_shift=ada_shift, ada_scale=ada_scale, ada_gate=ada_gate, router=router, expert_up=expert_up, expert_down=expert_down, picked_ids=picked_ids, out_grad=out_grad)


GELU_C = 0.7978845608028654

def gelu_tanh(values):
    inner_arg = GELU_C * (values + 0.044715 * values * values * values)
    return 0.5 * values * (1.0 + jnp.tanh(inner_arg))

def gelu_slope(values):
    inner_arg = GELU_C * (values + 0.044715 * values * values * values)
    tangent = jnp.tanh(inner_arg)
    return 0.5 * (1.0 + tangent) + 0.5 * values * (1.0 - tangent * tangent) * GELU_C * (1.0 + 3.0 * 0.044715 * values * values)

def reference(tokens, ada_shift, ada_scale, ada_gate, router, expert_up, expert_down, picked_ids, out_grad):
    inputs = tokens.astype(jnp.float32)
    centered = inputs - lax.optimization_barrier(jnp.mean(inputs, axis=1, keepdims=True))
    inverse_std = lax.rsqrt(lax.optimization_barrier(jnp.mean(centered * centered, axis=1, keepdims=True)) + 1e-06)
    normed = centered * inverse_std
    hidden = (normed * (1.0 + ada_scale) + ada_shift).astype(jnp.bfloat16)
    mixture = jnp.zeros((TOKENS, D), jnp.float32)
    stored = []
    for owner_idx in range(N_EXP):
        for slot_index in range(PAIR):
            token_ids = picked_ids[owner_idx, slot_index]
            column = router[owner_idx, :, slot_index]
            row_block = hidden[token_ids]
            logits = jnp.dot(row_block, column, preferred_element_type=jnp.float32)
            weights = jax.nn.sigmoid(logits)
            up_block = expert_up[owner_idx][:, slot_index * HID:(slot_index + 1) * HID]
            down_block = expert_down[owner_idx][slot_index * HID:(slot_index + 1) * HID]
            pre_act = jnp.dot(row_block, up_block, preferred_element_type=jnp.float32)
            activated = gelu_tanh(pre_act).astype(jnp.bfloat16)
            expert_out = jnp.dot(activated, down_block, preferred_element_type=jnp.float32)
            mixture = mixture.at[token_ids].add(weights[:, None] * expert_out)
            stored.append((token_ids, column, weights, row_block, up_block, down_block, pre_act, activated, expert_out))
    block_out = (inputs + ada_gate * mixture).astype(jnp.bfloat16)
    grad_in = out_grad.astype(jnp.float32)
    grad_mix = ada_gate * grad_in
    gate_grad = lax.optimization_barrier(jnp.sum(grad_in * mixture, axis=0))
    grad_hidden = jnp.zeros((TOKENS, D), jnp.float32)
    up_list = []
    down_list = []
    router_list = []
    for owner_idx in range(N_EXP):
        up_parts = []
        down_parts = []
        router_parts = []
        for slot_index in range(PAIR):
            token_ids, column, weights, row_block, up_block, down_block, pre_act, activated, expert_out = stored[owner_idx * PAIR + slot_index]
            mix_rows = grad_mix[token_ids]
            grad_rows = (weights[:, None] * mix_rows).astype(jnp.bfloat16)
            grad_weight = lax.optimization_barrier(jnp.sum(mix_rows * expert_out, axis=1))
            grad_logit = grad_weight * weights * (1.0 - weights)
            grad_act = jnp.dot(grad_rows, down_block.T, preferred_element_type=jnp.float32)
            grad_pre = (grad_act * gelu_slope(pre_act)).astype(jnp.bfloat16)
            down_parts.append(jnp.dot(activated.T, grad_rows, preferred_element_type=jnp.float32).astype(jnp.bfloat16))
            up_parts.append(jnp.dot(row_block.T, grad_pre, preferred_element_type=jnp.float32).astype(jnp.bfloat16))
            back_sum = jnp.dot(grad_pre, up_block.T, preferred_element_type=jnp.float32)
            grad_hidden = grad_hidden.at[token_ids].add(back_sum + grad_logit[:, None] * column.astype(jnp.float32)[None, :])
            router_parts.append(lax.optimization_barrier(jnp.sum(grad_logit[:, None] * row_block.astype(jnp.float32), axis=0)))
        up_list.append(jnp.concatenate(up_parts, axis=1))
        down_list.append(jnp.concatenate(down_parts, axis=0))
        router_list.append(jnp.stack(router_parts, axis=1))
    shift_grad = lax.optimization_barrier(jnp.sum(grad_hidden, axis=0))
    scale_grad = lax.optimization_barrier(jnp.sum(grad_hidden * normed, axis=0))
    grad_norm = grad_hidden * (1.0 + ada_scale)
    tokens_grad = (grad_in + inverse_std * (grad_norm - lax.optimization_barrier(jnp.mean(grad_norm, axis=1, keepdims=True)) - normed * lax.optimization_barrier(jnp.mean(grad_norm * normed, axis=1, keepdims=True)))).astype(jnp.bfloat16)
    up_grad = jnp.stack(up_list)
    down_grad = jnp.stack(down_list)
    router_grad = jnp.stack(router_list)
    return (block_out, tokens_grad, up_grad, down_grad, router_grad, shift_grad, scale_grad, gate_grad)
```

```python
import jax
import jax.numpy as jnp
from jax import lax
from jax.experimental import pallas as pl
from jax.experimental.pallas import tpu as pltpu
from jax.sharding import PartitionSpec as P

GELU_C = 0.7978845608028654
MESH = pl.DeviceIdType.MESH
F32 = jnp.float32
BF16 = jnp.bfloat16

D = 4096
HU = 512
TOK = 128
MOST = 8
NF = 2
F = D // NF
TILE = 512
SLOTS = 32 * MOST


def dot(a, b, ca, cb):
    return lax.dot_general(a, b, (((ca,), (cb,)), ((), ())), preferred_element_type=F32)


def exchange_kernel(
    tok_hbm,
    og_hbm,
    shift_ref,
    scale_ref,
    gate_ref,
    router_ref,
    up_hbm,
    down_hbm,
    picks_ref,
    block_hbm,
    tgrad_hbm,
    rows_hbm,
    grads_hbm,
    act_hbm,
    gp_hbm,
    vec_ref,
    tok,
    og,
    up,
    down,
    own,
    got,
    relay,
    rowmat,
    pre,
    gact,
    act,
    gpre,
    part,
    swap,
    first,
    mid,
    second,
    fin,
    slots,
    tables,
    mix,
    hid16,
    n64,
    og64,
    g64,
    c64,
    outb,
    outt,
    vparts,
    vin,
    vsum,
    gvec,
    loc,
    tab_s,
    tab_r,
    a1s,
    a1r,
    a2s,
    a2r,
    acs,
    acr,
    bcs,
    bcr,
    b1s,
    b1r,
    b2s,
    b2r,
    xs,
    xr,
    v1s,
    v1r,
    v2s,
    v2r,
):
    me = lax.axis_index("ctx")
    x = lax.axis_index("exp")
    z, y, c = me // 8, (me // 2) % 4, me % 2
    oc = 1 - c
    j = z // 2
    jo = 1 - j
    mate = (1 - z % 2) * 2

    def dev(zz, yy, cc, xx):
        return ((zz * 4 + yy) * 2 + cc, xx)

    def nxt(v, k):
        return (v + k) % 4

    pending = []

    def send(src, dst, ss, rs, to):
        cp = pltpu.make_async_remote_copy(
            src_ref=src, dst_ref=dst, send_sem=ss, recv_sem=rs, device_id=to, device_id_type=MESH
        )
        cp.start()
        pending.append(cp)
        return cp

    def local(src, dst, sem):
        cp = pltpu.make_async_copy(src, dst, sem)
        cp.start()
        return cp

    in_tok = local(tok_hbm, tok, loc.at[0])
    in_og = local(og_hbm, og, loc.at[1])
    in_up = local(up_hbm.at[0], up, loc.at[2])
    in_down = local(down_hbm.at[0], down, loc.at[3])

    bar = pltpu.get_barrier_semaphore()
    for k in range(1, 32):
        pl.semaphore_signal(bar, inc=1, device_id=((me + k) % 32, x), device_id_type=MESH)
    for k in range(1, 4):
        pl.semaphore_signal(bar, inc=1, device_id=(me, nxt(x, k)), device_id_type=MESH)

    lanes = lax.broadcasted_iota(jnp.int32, (MOST, TOK), 1)
    subl = lax.broadcasted_iota(jnp.int32, (MOST, TOK), 0)
    tri = (
        lax.broadcasted_iota(jnp.int32, (TOK, TOK), 0) <= lax.broadcasted_iota(jnp.int32, (TOK, TOK), 1)
    ).astype(F32).astype(BF16)
    tabs = []
    for jj in range(2):
        ids = jnp.broadcast_to(picks_ref[jj : jj + 1, :], (MOST, TOK)) - me * TOK
        inside = (ids >= 0) & (ids < TOK)
        inside_f = jnp.where(inside, 1.0, 0.0)
        count = dot(inside_f.astype(BF16), tri, 1, 0)
        hit = jnp.where(inside & (count == (subl + 1).astype(F32)), 1.0, 0.0)
        where_tok = jnp.sum(hit * ids.astype(F32), axis=1, keepdims=True)
        there = jnp.sum(hit, axis=1, keepdims=True)
        tabs.append(jnp.where((where_tok == lanes.astype(F32)) & (there > 0.5), 1.0, 0.0))
    table = jnp.concatenate(tabs, axis=0).astype(BF16)
    tables[x] = table

    in_tok.wait()
    trow = dot(table, tok[...], 1, 0)
    cen = trow - jnp.mean(trow, axis=1, keepdims=True)
    inv = lax.rsqrt(jnp.mean(cen * cen, axis=1, keepdims=True) + 1e-06)
    row_there = jnp.sum(table.astype(F32), axis=1, keepdims=True)
    hid = ((cen * inv * (1.0 + scale_ref[...]) + shift_ref[...]) * row_there).astype(BF16)
    hid16[...] = hid
    hidf = hid.astype(F32)
    rout = router_ref[...].astype(F32)
    logits = jnp.concatenate(
        [
            jnp.sum(hidf[MOST * jj : MOST * jj + MOST] * rout[jj : jj + 1], axis=1, keepdims=True)
            for jj in range(2)
        ],
        axis=0,
    )
    weight = 1.0 / (1.0 + jnp.exp(-logits))
    for f in range(NF):
        for jj in range(2):
            own[0, f, jj] = hidf[MOST * jj : MOST * jj + MOST, f * F : f * F + F].astype(BF16)
    in_og.wait()
    mixv = dot(table, og[...], 1, 0) * gate_ref[...]
    mix[...] = mixv
    gradv = weight * mixv
    for f in range(NF):
        for jj in range(2):
            own[1, f, jj] = gradv[MOST * jj : MOST * jj + MOST, f * F : f * F + F].astype(BF16)

    pl.semaphore_wait(bar, 34)

    tabc = [
        send(tables.at[x], tables.at[x], tab_s.at[k - 1], tab_r.at[k - 1], (me, nxt(x, k)))
        for k in range(1, 4)
    ]

    def recv(cps):
        for cp in cps:
            cp.wait_recv()

    def zfirst(f):
        return f % 2 == 0

    def gather1(a, f):
        if zfirst(f):
            return [
                send(
                    own.at[a, f, nxt(z, k) // 2],
                    got.at[a, f, c, y, z],
                    a1s.at[a, f, k - 1],
                    a1r.at[a, f, k - 1],
                    dev(nxt(z, k), y, c, x),
                )
                for k in range(1, 4)
            ]
        return [
            send(
                own.at[a, f],
                relay.at[a, f // 2, y],
                a1s.at[a, f, k - 1],
                a1r.at[a, f, k - 1],
                dev(z, nxt(y, k), c, x),
            )
            for k in range(1, 4)
        ]

    def gather2(a, f, g1):
        if zfirst(f):
            got[a, f, c, y, z] = own[a, f, j]
            recv(g1)
            return [
                send(
                    got.at[a, f, c, y],
                    got.at[a, f, c, y],
                    a2s.at[a, f, k - 1],
                    a2r.at[a, f, k - 1],
                    dev(z, nxt(y, k), c, x),
                )
                for k in range(1, 4)
            ]
        relay[a, f // 2, y] = own[a, f]
        recv(g1)
        cps = [
            send(
                relay.at[a, f // 2, :, nxt(z, k) // 2],
                got.at[a, f, c, :, z],
                a2s.at[a, f, k - 1],
                a2r.at[a, f, k - 1],
                dev(nxt(z, k), y, c, x),
            )
            for k in range(1, 4)
        ]
        got[a, f, c, :, z] = relay[a, f // 2, :, j]
        return cps

    def gather3(a, f, g2):
        recv(g2)
        return send(
            got.at[a, f, c], got.at[a, f, c], acs.at[a, f], acr.at[a, f], dev(z, y, oc, x)
        )

    def rows_ready(a, f, g3):
        g3.wait_recv()

        def pair(i, _):
            cc, yy, zz = i // 8, (i // 2) % 4, (i % 2) * 2
            two = got[a, f, cc, yy, pl.ds(zz, 2)].astype(F32).reshape(16, F)
            rowmat[a, pl.ds(pl.multiple_of(i * 16, 16), 16), f * F : f * F + F] = two.astype(BF16)
            return 0

        lax.fori_loop(0, 16, pair, 0)

    def partial(a, f):
        left = (act if a == 0 else gpre)[...]
        for t in range(F // TILE):
            lo = f * F + t * TILE
            if a == 0:
                prod = dot(left, down[:, lo : lo + TILE], 1, 0)
            else:
                prod = dot(left, up[lo : lo + TILE, :], 1, 1)
            part[a, f, :, :, :, :, t * TILE : t * TILE + TILE] = prod.reshape(
                2, 4, 4, MOST, TILE
            ).astype(BF16)
        return send(part.at[a, f, oc], swap.at[a, f], bcs.at[a, f], bcr.at[a, f], dev(z, y, oc, x))

    def return1(a, f, cp):
        cp.wait_recv()

        def add(i, _):
            yy, zz = i // 4, i % 4
            swap[a, f, yy, zz] = (
                swap[a, f, yy, zz].astype(F32) + part[a, f, c, yy, zz].astype(F32)
            ).astype(BF16)
            return 0

        lax.fori_loop(0, 16, add, 0)
        if zfirst(f):
            return [
                send(
                    swap.at[a, f, nxt(y, k)],
                    first.at[a, f, k - 1],
                    b1s.at[a, f, k - 1],
                    b1r.at[a, f, k - 1],
                    dev(z, nxt(y, k), c, x),
                )
                for k in range(1, 4)
            ]
        return [
            send(
                swap.at[a, f, :, nxt(z, k)],
                first.at[a, f, k - 1],
                b1s.at[a, f, k - 1],
                b1r.at[a, f, k - 1],
                dev(nxt(z, k), y, c, x),
            )
            for k in range(1, 4)
        ]

    def return2(a, f, cps):
        recv(cps)
        if zfirst(f):

            def add(i, _):
                mid[a, f, i] = (
                    swap[a, f, y, i].astype(F32)
                    + first[a, f, 0, i].astype(F32)
                    + first[a, f, 1, i].astype(F32)
                    + first[a, f, 2, i].astype(F32)
                ).astype(BF16)
                return 0

            lax.fori_loop(0, 4, add, 0)
            return [
                send(
                    mid.at[a, f, nxt(z, k)],
                    second.at[a, f, k - 1, 0],
                    b2s.at[a, f, k - 1],
                    b2r.at[a, f, k - 1],
                    dev(nxt(z, k), y, c, x),
                )
                for k in range(1, 4)
            ]

        def add(i, _):
            mid[a, f, 2 * i + j] = (
                swap[a, f, i, z].astype(F32) + first[a, f, mate, i].astype(F32)
            ).astype(BF16)
            mid[a, f, 2 * i + jo] = (
                first[a, f, 1, i].astype(F32) + first[a, f, 2 - mate, i].astype(F32)
            ).astype(BF16)
            return 0

        lax.fori_loop(0, 4, add, 0)
        return [
            send(
                mid.at[a, f, pl.ds(2 * nxt(y, k), 2)],
                second.at[a, f, k - 1],
                b2s.at[a, f, k - 1],
                b2r.at[a, f, k - 1],
                dev(z, nxt(y, k), c, x),
            )
            for k in range(1, 4)
        ]

    def return3(a, f, cps):
        recv(cps)
        if zfirst(f):
            fin[j] = mid[a, f, z].astype(F32) + second[a, f, mate, 0].astype(F32)
            fin[jo] = second[a, f, 1, 0].astype(F32) + second[a, f, 2 - mate, 0].astype(F32)
        else:
            fin[...] = (
                mid[a, f, pl.ds(2 * y, 2)].astype(F32)
                + second[a, f, 0].astype(F32)
                + second[a, f, 1].astype(F32)
                + second[a, f, 2].astype(F32)
            )
        return fin[...].reshape(2 * MOST, F)

    def to_x(a, f, rows):
        slots[a, f, x] = rows.reshape(2, MOST, F).astype(BF16)
        return [
            send(
                slots.at[a, f, x],
                slots.at[a, f, x],
                xs.at[a, f, k - 1],
                xr.at[a, f, k - 1],
                (me, nxt(x, k)),
            )
            for k in range(1, 4)
        ]

    units = [(a, f) for a in range(2) for f in range(NF)]
    g1 = {u: gather1(*u) for u in units}
    g2, g3 = {}, {}
    for u in units:
        g2[u] = gather2(*u, g1[u])

    recv(tabc)
    tab64 = tables[...].astype(F32).reshape(64, TOK).T.astype(BF16)
    for q in range(4):
        sl = slice(16 * q, 16 * q + 16)
        t16 = dot(tables[q], tok[...], 1, 0)
        c16 = t16 - jnp.mean(t16, axis=1, keepdims=True)
        i16 = lax.rsqrt(jnp.mean(c16 * c16, axis=1, keepdims=True) + 1e-06)
        n64[sl, :] = c16 * i16
        og64[sl, :] = dot(tables[q], og[...], 1, 0).astype(BF16)

    for f in range(NF):
        g3[0, f] = gather3(0, f, g2[0, f])
    in_up.wait()
    for f in range(NF):
        rows_ready(0, f, g3[0, f])
        acc = dot(rowmat[0, :, f * F : f * F + F], up[f * F : f * F + F, :], 1, 0)
        pre[...] = acc if f == 0 else pre[...] + acc
    prev = pre[...]
    tang = jnp.tanh(GELU_C * (prev + 0.044715 * prev * prev * prev))
    act[...] = (0.5 * prev * (1.0 + tang)).astype(BF16)
    pre[...] = 0.5 * (1.0 + tang) + 0.5 * prev * (1.0 - tang * tang) * GELU_C * (
        1.0 + 3.0 * 0.044715 * prev * prev
    )
    outs = [local(rowmat.at[0], rows_hbm, loc.at[4]), local(act, act_hbm, loc.at[5])]
    in_down.wait()
    r0, r1, r2, r3 = {}, {}, {}, {}
    for f in range(NF):
        r0[0, f] = partial(0, f)
    for f in range(NF):
        g3[1, f] = gather3(1, f, g2[1, f])
    for f in range(NF):
        r1[0, f] = return1(0, f, r0[0, f])
    for f in range(NF):
        rows_ready(1, f, g3[1, f])
        acc = dot(rowmat[1, :, f * F : f * F + F], down[:, f * F : f * F + F], 1, 1)
        gact[...] = acc if f == 0 else gact[...] + acc
    gpre[...] = (gact[...] * pre[...]).astype(BF16)
    outs += [local(rowmat.at[1], grads_hbm, loc.at[6]), local(gpre, gp_hbm, loc.at[7])]
    for f in range(NF):
        r0[1, f] = partial(1, f)
    for f in range(NF):
        r2[0, f] = return2(0, f, r1[0, f])
    for f in range(NF):
        r1[1, f] = return1(1, f, r0[1, f])
    grad_w = jnp.zeros((2 * MOST, 1), F32)
    for f in range(NF):
        rows = return3(0, f, r2[0, f])
        grad_w = grad_w + jnp.sum(rows * mix[:, f * F : f * F + F], axis=1, keepdims=True)
        r3[0, f] = to_x(0, f, rows * weight)
    grad_logit = grad_w * weight * (1.0 - weight)
    for f in range(NF):
        r2[1, f] = return2(1, f, r1[1, f])
    row8 = lax.broadcasted_iota(jnp.int32, (8, F), 0)
    for f in range(NF):
        cols = slice(f * F, f * F + F)
        recv(r3[0, f])
        outrows = slots[0, f].astype(F32).reshape(64, F)
        gate_sum = jnp.sum(outrows * og64[:, cols].astype(F32), axis=0, keepdims=True)
        hg = hid16[:, cols].astype(F32) * grad_logit
        gvec[:, cols] = jnp.where(
            row8 == 2,
            gate_sum,
            jnp.where(
                row8 == 3,
                jnp.sum(hg[:MOST], axis=0, keepdims=True),
                jnp.where(row8 == 4, jnp.sum(hg[MOST:], axis=0, keepdims=True), 0.0),
            ),
        )
        outb[:, cols] = (
            tok[:, cols].astype(F32) + gate_ref[:, cols] * dot(tab64, outrows.astype(BF16), 1, 0)
        ).astype(BF16)
    outs += [local(outb, block_hbm, loc.at[8])]
    for f in range(NF):
        rows = return3(1, f, r2[1, f])
        add = [
            grad_logit[MOST * jj : MOST * jj + MOST]
            * router_ref[jj : jj + 1, f * F : f * F + F].astype(F32)
            for jj in range(2)
        ]
        r3[1, f] = to_x(1, f, rows + jnp.concatenate(add, axis=0))
    m1 = jnp.zeros((64, 1), F32)
    m2 = jnp.zeros((64, 1), F32)
    for f in range(NF):
        cols = slice(f * F, f * F + F)
        recv(r3[1, f])
        gh = slots[1, f].astype(F32).reshape(64, F)
        ghn = gh * n64[:, cols]
        gvec[:, cols] = jnp.where(
            row8 == 0,
            jnp.sum(gh, axis=0, keepdims=True),
            jnp.where(row8 == 1, jnp.sum(ghn, axis=0, keepdims=True), gvec[:, cols]),
        )
        one = 1.0 + scale_ref[:, cols]
        g64[:, cols] = gh * one
        m1 = m1 + jnp.sum(gh * one, axis=1, keepdims=True)
        m2 = m2 + jnp.sum(ghn * one, axis=1, keepdims=True)
    for d in range(32):
        vparts[d] = gvec[:, d * 128 : d * 128 + 128]
    v1 = []
    for k in range(1, 32):
        to = (me + k) % 32
        v1.append(send(vparts.at[to], vin.at[me], v1s.at[k - 1], v1r.at[k - 1], (to, x)))
    vin[me] = vparts[me]
    m1 = m1 * (1.0 / D)
    m2 = m2 * (1.0 / D)
    for q in range(4):
        sl = slice(16 * q, 16 * q + 16)
        t16 = dot(tables[q], tok[...], 1, 0)
        c16 = t16 - jnp.mean(t16, axis=1, keepdims=True)
        i16 = lax.rsqrt(jnp.mean(c16 * c16, axis=1, keepdims=True) + 1e-06)
        c64[sl, :] = (i16 * (g64[sl, :] - m1[sl] - n64[sl, :] * m2[sl])).astype(BF16)
    for t in range(D // TILE):
        cols = slice(t * TILE, t * TILE + TILE)
        outt[:, cols] = (og[:, cols].astype(F32) + dot(tab64, c64[:, cols], 1, 0)).astype(BF16)
    outs += [local(outt, tgrad_hbm, loc.at[9])]
    recv(v1)
    total = vin[0]
    for d in range(1, 32):
        total = total + vin[d]
    vsum[me] = total
    v2 = []
    for k in range(1, 32):
        to = (me + k) % 32
        v2.append(send(vsum.at[me], vsum.at[me], v2s.at[k - 1], v2r.at[k - 1], (to, x)))
    recv(v2)
    for d in range(32):
        vec_ref[:, d * 128 : d * 128 + 128] = vsum[d]
    for cp in outs:
        cp.wait()
    for cp in pending:
        cp.wait_send()


def weight_grads_kernel(rows_ref, grads_ref, act_ref, gp_ref, up_ref, down_ref):
    up_ref[0] = dot(rows_ref[...], gp_ref[...], 0, 0).astype(BF16)
    down_ref[0] = dot(act_ref[...], grads_ref[...], 0, 0).astype(BF16)


def per_device(tokens, shift, scale, gate, router, up, down, picks, out_grad):
    hbm = pl.BlockSpec(memory_space=pl.ANY)
    vmem = pl.BlockSpec(memory_space=pltpu.VMEM)
    dma = pltpu.SemaphoreType.DMA
    shape = jax.ShapeDtypeStruct
    block, tgrad, rows, grads, act, gp, vec = pl.pallas_call(
        exchange_kernel,
        out_shape=(
            shape((TOK, D), BF16),
            shape((TOK, D), BF16),
            shape((SLOTS, D), BF16),
            shape((SLOTS, D), BF16),
            shape((SLOTS, HU), BF16),
            shape((SLOTS, HU), BF16),
            shape((8, D), F32),
        ),
        in_specs=[hbm, hbm, vmem, vmem, vmem, vmem, hbm, hbm, vmem],
        out_specs=(hbm, hbm, hbm, hbm, hbm, hbm, vmem),
        scratch_shapes=[
            pltpu.VMEM((TOK, D), BF16),
            pltpu.VMEM((TOK, D), BF16),
            pltpu.VMEM((D, HU), BF16),
            pltpu.VMEM((HU, D), BF16),
            pltpu.VMEM((2, NF, 2, MOST, F), BF16),
            pltpu.VMEM((2, NF, 2, 4, 4, MOST, F), BF16),
            pltpu.VMEM((2, NF // 2, 4, 2, MOST, F), BF16),
            pltpu.VMEM((2, SLOTS, D), BF16),
            pltpu.VMEM((SLOTS, HU), F32),
            pltpu.VMEM((SLOTS, HU), F32),
            pltpu.VMEM((SLOTS, HU), BF16),
            pltpu.VMEM((SLOTS, HU), BF16),
            pltpu.VMEM((2, NF, 2, 4, 4, MOST, F), BF16),
            pltpu.VMEM((2, NF, 4, 4, MOST, F), BF16),
            pltpu.VMEM((2, NF, 3, 4, MOST, F), BF16),
            pltpu.VMEM((2, NF, 8, MOST, F), BF16),
            pltpu.VMEM((2, NF, 3, 2, MOST, F), BF16),
            pltpu.VMEM((2, MOST, F), F32),
            pltpu.VMEM((2, NF, 4, 2, MOST, F), BF16),
            pltpu.VMEM((4, 2 * MOST, TOK), BF16),
            pltpu.VMEM((2 * MOST, D), F32),
            pltpu.VMEM((2 * MOST, D), BF16),
            pltpu.VMEM((64, D), F32),
            pltpu.VMEM((64, D), BF16),
            pltpu.VMEM((64, D), F32),
            pltpu.VMEM((64, D), BF16),
            pltpu.VMEM((TOK, D), BF16),
            pltpu.VMEM((TOK, D), BF16),
            pltpu.VMEM((32, 8, 128), F32),
            pltpu.VMEM((32, 8, 128), F32),
            pltpu.VMEM((32, 8, 128), F32),
            pltpu.VMEM((8, D), F32),
            dma((10,)),
            dma((3,)),
            dma((3,)),
            dma((2, NF, 3)),
            dma((2, NF, 3)),
            dma((2, NF, 3)),
            dma((2, NF, 3)),
            dma((2, NF)),
            dma((2, NF)),
            dma((2, NF)),
            dma((2, NF)),
            dma((2, NF, 3)),
            dma((2, NF, 3)),
            dma((2, NF, 3)),
            dma((2, NF, 3)),
            dma((2, NF, 3)),
            dma((2, NF, 3)),
            dma((31,)),
            dma((31,)),
            dma((31,)),
            dma((31,)),
        ],
        compiler_params=pltpu.CompilerParams(
            collective_id=0, has_side_effects=True, vmem_limit_bytes=56 * 2**20
        ),
        cost_estimate=pl.CostEstimate(
            flops=12 * SLOTS * D * HU, bytes_accessed=24 * 2**20, transcendentals=SLOTS * HU
        ),
    )(
        tokens,
        out_grad,
        shift.reshape(1, D),
        scale.reshape(1, D),
        gate.reshape(1, D),
        router[0].T,
        up,
        down,
        picks[0],
    )
    steps = D // TILE
    full = pl.BlockSpec((SLOTS, HU), lambda i: (0, 0))
    cut = pl.BlockSpec((SLOTS, TILE), lambda i: (0, i))
    up_grad, down_grad = pl.pallas_call(
        weight_grads_kernel,
        grid=(steps,),
        out_shape=(shape((1, D, HU), BF16), shape((1, HU, D), BF16)),
        in_specs=[cut, cut, full, full],
        out_specs=(
            pl.BlockSpec((1, TILE, HU), lambda i: (0, i, 0)),
            pl.BlockSpec((1, HU, TILE), lambda i: (0, 0, i)),
        ),
        cost_estimate=pl.CostEstimate(
            flops=4 * SLOTS * D * HU, bytes_accessed=13 * 2**20, transcendentals=0
        ),
    )(rows, grads, act, gp)
    return (
        block,
        tgrad,
        up_grad,
        down_grad,
        vec[3:5].T[None],
        vec[0],
        vec[1],
        vec[2],
    )


def solution(mesh):
    in_specs = (
        P("ctx", None),
        P(),
        P(),
        P(),
        P("exp", None, None),
        P("exp", None, "ctx"),
        P("exp", "ctx", None),
        P("exp", None, None),
        P("ctx", None),
    )
    out_specs = (
        P("ctx", None),
        P("ctx", None),
        P("exp", None, "ctx"),
        P("exp", "ctx", None),
        P("exp", None, None),
        P(),
        P(),
        P(),
    )
    return jax.shard_map(
        per_device, mesh=mesh, in_specs=in_specs, out_specs=out_specs, check_vma=False
    )
```

```python
import jax
import jax.numpy as jnp
from jax import lax
from jax.experimental import pallas as pl
from jax.experimental.pallas import tpu as pltpu
from jax.sharding import PartitionSpec as P

GELU_C = 0.7978845608028654
MESH = pl.DeviceIdType.MESH
F32 = jnp.float32
BF16 = jnp.bfloat16

D = 4096
HU = 512
TOK = 128
MOST = 8
NF = 2
F = D // NF
TILE = 512
SLOTS = 32 * MOST


def dot(a, b, ca, cb):
    return lax.dot_general(a, b, (((ca,), (cb,)), ((), ())), preferred_element_type=F32)


def exchange_kernel(
    tok_hbm,
    og_hbm,
    shift_ref,
    scale_ref,
    gate_ref,
    router_ref,
    up_hbm,
    down_hbm,
    picks_ref,
    rows_hbm,
    grads_hbm,
    act_hbm,
    gp_hbm,
    mixrows_hbm,
    corr_hbm,
    table_ref,
    vec_ref,
    tok,
    og,
    up,
    down,
    own,
    got,
    relay,
    rowmat,
    pre,
    gact,
    act,
    gpre,
    part,
    swap,
    first,
    mid,
    second,
    fin,
    slots,
    tables,
    mix,
    hid16,
    n64,
    og64,
    g64,
    c64,
    x64,
    vsrc,
    vswap,
    vy,
    vz,
    vfin,
    loc,
    tab_s,
    tab_r,
    a1s,
    a1r,
    a2s,
    a2r,
    acs,
    acr,
    bcs,
    bcr,
    b1s,
    b1r,
    b2s,
    b2r,
    xs,
    xr,
    vs,
    vr,
):
    me = lax.axis_index("ctx")
    x = lax.axis_index("exp")
    z, y, c = me // 8, (me // 2) % 4, me % 2
    oc = 1 - c
    j = z // 2
    jo = 1 - j
    mate = (1 - z % 2) * 2

    def dev(zz, yy, cc, xx):
        return ((zz * 4 + yy) * 2 + cc, xx)

    def nxt(v, k):
        return (v + k) % 4

    pending = []

    def send(src, dst, ss, rs, to):
        cp = pltpu.make_async_remote_copy(
            src_ref=src, dst_ref=dst, send_sem=ss, recv_sem=rs, device_id=to, device_id_type=MESH
        )
        cp.start()
        pending.append(cp)
        return cp

    def local(src, dst, sem):
        cp = pltpu.make_async_copy(src, dst, sem)
        cp.start()
        return cp

    in_tok = local(tok_hbm, tok, loc.at[0])
    in_og = local(og_hbm, og, loc.at[1])
    in_up = local(up_hbm.at[0], up, loc.at[2])
    in_down = local(down_hbm.at[0], down, loc.at[3])

    bar = pltpu.get_barrier_semaphore()
    pl.semaphore_signal(bar, inc=1, device_id=dev(z, y, oc, x), device_id_type=MESH)
    for k in range(1, 4):
        pl.semaphore_signal(bar, inc=1, device_id=dev(nxt(z, k), y, c, x), device_id_type=MESH)
        pl.semaphore_signal(bar, inc=1, device_id=dev(z, nxt(y, k), c, x), device_id_type=MESH)
        pl.semaphore_signal(bar, inc=1, device_id=(me, nxt(x, k)), device_id_type=MESH)

    lanes = lax.broadcasted_iota(jnp.int32, (MOST, TOK), 1)
    subl = lax.broadcasted_iota(jnp.int32, (MOST, TOK), 0)
    tri = (
        lax.broadcasted_iota(jnp.int32, (TOK, TOK), 0) <= lax.broadcasted_iota(jnp.int32, (TOK, TOK), 1)
    ).astype(F32).astype(BF16)
    tabs = []
    for jj in range(2):
        ids = jnp.broadcast_to(picks_ref[jj : jj + 1, :], (MOST, TOK)) - me * TOK
        inside = (ids >= 0) & (ids < TOK)
        inside_f = jnp.where(inside, 1.0, 0.0)
        count = dot(inside_f.astype(BF16), tri, 1, 0)
        hit = jnp.where(inside & (count == (subl + 1).astype(F32)), 1.0, 0.0)
        where_tok = jnp.sum(hit * ids.astype(F32), axis=1, keepdims=True)
        there = jnp.sum(hit, axis=1, keepdims=True)
        tabs.append(jnp.where((where_tok == lanes.astype(F32)) & (there > 0.5), 1.0, 0.0))
    table = jnp.concatenate(tabs, axis=0).astype(BF16)
    tables[x] = table

    in_tok.wait()
    trow = dot(table, tok[...], 1, 0)
    cen = trow - jnp.mean(trow, axis=1, keepdims=True)
    inv = lax.rsqrt(jnp.mean(cen * cen, axis=1, keepdims=True) + 1e-06)
    row_there = jnp.sum(table.astype(F32), axis=1, keepdims=True)
    hid = ((cen * inv * (1.0 + scale_ref[...]) + shift_ref[...]) * row_there).astype(BF16)
    hid16[...] = hid
    hidf = hid.astype(F32)
    rout = router_ref[...].astype(F32)
    logits = jnp.concatenate(
        [
            jnp.sum(hidf[MOST * jj : MOST * jj + MOST] * rout[jj : jj + 1], axis=1, keepdims=True)
            for jj in range(2)
        ],
        axis=0,
    )
    weight = 1.0 / (1.0 + jnp.exp(-logits))
    for f in range(NF):
        for jj in range(2):
            own[0, f, jj] = hidf[MOST * jj : MOST * jj + MOST, f * F : f * F + F].astype(BF16)
    in_og.wait()
    mixv = dot(table, og[...], 1, 0) * gate_ref[...]
    mix[...] = mixv
    gradv = weight * mixv
    for f in range(NF):
        for jj in range(2):
            own[1, f, jj] = gradv[MOST * jj : MOST * jj + MOST, f * F : f * F + F].astype(BF16)

    pl.semaphore_wait(bar, 10)

    tabc = [
        send(tables.at[x], tables.at[x], tab_s.at[k - 1], tab_r.at[k - 1], (me, nxt(x, k)))
        for k in range(1, 4)
    ]

    def recv(cps):
        for cp in cps:
            cp.wait_recv()

    def zfirst(f):
        return f % 2 == 0

    def gather1(a, f):
        if zfirst(f):
            return [
                send(
                    own.at[a, f, nxt(z, k) // 2],
                    got.at[a, f, c, y, z],
                    a1s.at[a, f, k - 1],
                    a1r.at[a, f, k - 1],
                    dev(nxt(z, k), y, c, x),
                )
                for k in range(1, 4)
            ]
        return [
            send(
                own.at[a, f],
                relay.at[a, f // 2, y],
                a1s.at[a, f, k - 1],
                a1r.at[a, f, k - 1],
                dev(z, nxt(y, k), c, x),
            )
            for k in range(1, 4)
        ]

    def gather2(a, f, g1):
        if zfirst(f):
            got[a, f, c, y, z] = own[a, f, j]
            recv(g1)
            return [
                send(
                    got.at[a, f, c, y],
                    got.at[a, f, c, y],
                    a2s.at[a, f, k - 1],
                    a2r.at[a, f, k - 1],
                    dev(z, nxt(y, k), c, x),
                )
                for k in range(1, 4)
            ]
        relay[a, f // 2, y] = own[a, f]
        recv(g1)
        cps = [
            send(
                relay.at[a, f // 2, :, nxt(z, k) // 2],
                got.at[a, f, c, :, z],
                a2s.at[a, f, k - 1],
                a2r.at[a, f, k - 1],
                dev(nxt(z, k), y, c, x),
            )
            for k in range(1, 4)
        ]
        got[a, f, c, :, z] = relay[a, f // 2, :, j]
        return cps

    def gather3(a, f, g2):
        recv(g2)
        return send(
            got.at[a, f, c], got.at[a, f, c], acs.at[a, f], acr.at[a, f], dev(z, y, oc, x)
        )

    def rows_ready(a, f, g3):
        g3.wait_recv()

        def pair(i, _):
            cc, yy, zz = i // 8, (i // 2) % 4, (i % 2) * 2
            two = got[a, f, cc, yy, pl.ds(zz, 2)].astype(F32).reshape(16, F)
            rowmat[a, pl.ds(pl.multiple_of(i * 16, 16), 16), f * F : f * F + F] = two.astype(BF16)
            return 0

        lax.fori_loop(0, 16, pair, 0)

    def partial(a, f):
        left = (act if a == 0 else gpre)[...]
        for t in range(F // TILE):
            lo = f * F + t * TILE
            if a == 0:
                prod = dot(left, down[:, lo : lo + TILE], 1, 0)
            else:
                prod = dot(left, up[lo : lo + TILE, :], 1, 1)
            part[a, f, :, :, :, :, t * TILE : t * TILE + TILE] = prod.reshape(
                2, 4, 4, MOST, TILE
            ).astype(BF16)
        return send(part.at[a, f, oc], swap.at[a, f], bcs.at[a, f], bcr.at[a, f], dev(z, y, oc, x))

    def return1(a, f, cp):
        cp.wait_recv()

        def add(i, _):
            yy, zz = i // 4, i % 4
            swap[a, f, yy, zz] = (
                swap[a, f, yy, zz].astype(F32) + part[a, f, c, yy, zz].astype(F32)
            ).astype(BF16)
            return 0

        lax.fori_loop(0, 16, add, 0)
        if zfirst(f):
            return [
                send(
                    swap.at[a, f, nxt(y, k)],
                    first.at[a, f, k - 1],
                    b1s.at[a, f, k - 1],
                    b1r.at[a, f, k - 1],
                    dev(z, nxt(y, k), c, x),
                )
                for k in range(1, 4)
            ]
        return [
            send(
                swap.at[a, f, :, nxt(z, k)],
                first.at[a, f, k - 1],
                b1s.at[a, f, k - 1],
                b1r.at[a, f, k - 1],
                dev(nxt(z, k), y, c, x),
            )
            for k in range(1, 4)
        ]

    def return2(a, f, cps):
        recv(cps)
        if zfirst(f):

            def add(i, _):
                mid[a, f, i] = (
                    swap[a, f, y, i].astype(F32)
                    + first[a, f, 0, i].astype(F32)
                    + first[a, f, 1, i].astype(F32)
                    + first[a, f, 2, i].astype(F32)
                ).astype(BF16)
                return 0

            lax.fori_loop(0, 4, add, 0)
            return [
                send(
                    mid.at[a, f, nxt(z, k)],
                    second.at[a, f, k - 1, 0],
                    b2s.at[a, f, k - 1],
                    b2r.at[a, f, k - 1],
                    dev(nxt(z, k), y, c, x),
                )
                for k in range(1, 4)
            ]

        def add(i, _):
            mid[a, f, 2 * i + j] = (
                swap[a, f, i, z].astype(F32) + first[a, f, mate, i].astype(F32)
            ).astype(BF16)
            mid[a, f, 2 * i + jo] = (
                first[a, f, 1, i].astype(F32) + first[a, f, 2 - mate, i].astype(F32)
            ).astype(BF16)
            return 0

        lax.fori_loop(0, 4, add, 0)
        return [
            send(
                mid.at[a, f, pl.ds(2 * nxt(y, k), 2)],
                second.at[a, f, k - 1],
                b2s.at[a, f, k - 1],
                b2r.at[a, f, k - 1],
                dev(z, nxt(y, k), c, x),
            )
            for k in range(1, 4)
        ]

    def return3(a, f, cps):
        recv(cps)
        if zfirst(f):
            fin[j] = mid[a, f, z].astype(F32) + second[a, f, mate, 0].astype(F32)
            fin[jo] = second[a, f, 1, 0].astype(F32) + second[a, f, 2 - mate, 0].astype(F32)
        else:
            fin[...] = (
                mid[a, f, pl.ds(2 * y, 2)].astype(F32)
                + second[a, f, 0].astype(F32)
                + second[a, f, 1].astype(F32)
                + second[a, f, 2].astype(F32)
            )
        return fin[...].reshape(2 * MOST, F)

    def to_x(a, f, rows):
        slots[a, f, x] = rows.reshape(2, MOST, F).astype(BF16)
        return [
            send(
                slots.at[a, f, x],
                slots.at[a, f, x],
                xs.at[a, f, k - 1],
                xr.at[a, f, k - 1],
                (me, nxt(x, k)),
            )
            for k in range(1, 4)
        ]

    def spread(row, stage, cc, n):
        for i in range(D // TILE):
            vsrc[stage, cc, n, i : i + 1, :] = row[:, i * TILE : i * TILE + TILE]

    def vsum1(s, n):
        return send(
            vsrc.at[s, oc, pl.ds(0, n)],
            vswap.at[s, pl.ds(0, n)],
            vs.at[s, 0],
            vr.at[s, 0],
            dev(z, y, oc, x),
        )

    def vsum2(s, n, cp):
        cp.wait_recv()
        vy[s, y, pl.ds(0, n)] = vsrc[s, c, pl.ds(0, n)] + vswap[s, pl.ds(0, n)]
        return [
            send(
                vy.at[s, y, pl.ds(0, n)],
                vy.at[s, y, pl.ds(0, n)],
                vs.at[s, k],
                vr.at[s, k],
                dev(z, nxt(y, k), c, x),
            )
            for k in range(1, 4)
        ]

    def vsum3(s, n, cps):
        recv(cps)
        cut = pl.ds(0, n)
        vz[s, z, cut] = (vy[s, 0, cut] + vy[s, 1, cut]) + (vy[s, 2, cut] + vy[s, 3, cut])
        return [
            send(
                vz.at[s, z, cut],
                vz.at[s, z, cut],
                vs.at[s, 3 + k],
                vr.at[s, 3 + k],
                dev(nxt(z, k), y, c, x),
            )
            for k in range(1, 4)
        ]

    def vsum4(s, n, cps):
        recv(cps)
        cut = pl.ds(0, n)
        vfin[s, c, cut] = (vz[s, 0, cut] + vz[s, 1, cut]) + (vz[s, 2, cut] + vz[s, 3, cut])
        return send(
            vfin.at[s, c, cut], vfin.at[s, c, cut], vs.at[s, 7], vr.at[s, 7], dev(z, y, oc, x)
        )

    drained = [0]

    def drain():
        for cp in pending[drained[0] :]:
            cp.wait_send()
        drained[0] = len(pending)

    parts = range(NF)
    g1, g2, g3 = {}, {}, {}
    for f in parts:
        g1[0, f] = gather1(0, f)
    for f in parts:
        g2[0, f] = gather2(0, f, g1[0, f])
    for f in parts:
        g1[1, f] = gather1(1, f)

    recv(tabc)
    tabt = tables[...].astype(F32).reshape(64, TOK).T.astype(BF16)
    table_ref[...] = tabt
    invs = []
    for q in range(4):
        sl = slice(16 * q, 16 * q + 16)
        t16 = dot(tables[q], tok[...], 1, 0)
        c16 = t16 - jnp.mean(t16, axis=1, keepdims=True)
        i16 = lax.rsqrt(jnp.mean(c16 * c16, axis=1, keepdims=True) + 1e-06)
        invs.append(i16)
        n64[sl, :] = c16 * i16
        og64[sl, :] = dot(tables[q], og[...], 1, 0).astype(BF16)

    for f in parts:
        g3[0, f] = gather3(0, f, g2[0, f])
        g2[1, f] = gather2(1, f, g1[1, f])
    in_up.wait()
    for f in parts:
        rows_ready(0, f, g3[0, f])
        acc = dot(rowmat[0, :, f * F : f * F + F], up[f * F : f * F + F, :], 1, 0)
        pre[...] = acc if f == 0 else pre[...] + acc
    prev = pre[...]
    tang = jnp.tanh(GELU_C * (prev + 0.044715 * prev * prev * prev))
    act[...] = (0.5 * prev * (1.0 + tang)).astype(BF16)
    pre[...] = 0.5 * (1.0 + tang) + 0.5 * prev * (1.0 - tang * tang) * GELU_C * (
        1.0 + 3.0 * 0.044715 * prev * prev
    )
    outs = [local(rowmat.at[0], rows_hbm, loc.at[4]), local(act, act_hbm, loc.at[5])]
    in_down.wait()
    r0, r1, r2, r3 = {}, {}, {}, {}
    for f in parts:
        r0[0, f] = partial(0, f)
    for f in parts:
        g3[1, f] = gather3(1, f, g2[1, f])
    for f in parts:
        r1[0, f] = return1(0, f, r0[0, f])
    for f in parts:
        rows_ready(1, f, g3[1, f])
        acc = dot(rowmat[1, :, f * F : f * F + F], down[:, f * F : f * F + F], 1, 1)
        gact[...] = acc if f == 0 else gact[...] + acc
    gpre[...] = (gact[...] * pre[...]).astype(BF16)
    outs += [local(rowmat.at[1], grads_hbm, loc.at[6]), local(gpre, gp_hbm, loc.at[7])]
    for f in parts:
        r0[1, f] = partial(1, f)
    for f in parts:
        r2[0, f] = return2(0, f, r1[0, f])
    for f in parts:
        r1[1, f] = return1(1, f, r0[1, f])
    grad_w = jnp.zeros((2 * MOST, 1), F32)
    for f in parts:
        rows = return3(0, f, r2[0, f])
        grad_w = grad_w + jnp.sum(rows * mix[:, f * F : f * F + F], axis=1, keepdims=True)
        r3[0, f] = to_x(0, f, rows * weight)
    grad_logit = grad_w * weight * (1.0 - weight)
    for f in parts:
        r2[1, f] = return2(1, f, r1[1, f])
    hg = hid16[...].astype(F32) * grad_logit
    spread(jnp.sum(hg[:MOST], axis=0, keepdims=True), 0, 0, 1)
    spread(jnp.sum(hg[MOST:], axis=0, keepdims=True), 0, 1, 0)
    vsrc[0, 1, 1] = jnp.zeros((8, TILE), F32)
    sums = []
    for f in parts:
        cols = slice(f * F, f * F + F)
        recv(r3[0, f])
        outrows = slots[0, f].astype(F32).reshape(64, F)
        sums.append(jnp.sum(outrows * og64[:, cols].astype(F32), axis=0, keepdims=True))
        x64[:, cols] = outrows.astype(BF16)
    spread(jnp.concatenate(sums, axis=1), 0, 0, 0)
    va = vsum1(0, 2)
    outs += [local(x64, mixrows_hbm, loc.at[8])]
    drain()
    for f in parts:
        rows = return3(1, f, r2[1, f])
        add = [
            grad_logit[MOST * jj : MOST * jj + MOST]
            * router_ref[jj : jj + 1, f * F : f * F + F].astype(F32)
            for jj in range(2)
        ]
        r3[1, f] = to_x(1, f, rows + jnp.concatenate(add, axis=0))
    vb = vsum2(0, 2, va)
    m1 = jnp.zeros((64, 1), F32)
    m2 = jnp.zeros((64, 1), F32)
    sums, sums_n = [], []
    for f in parts:
        cols = slice(f * F, f * F + F)
        recv(r3[1, f])
        gh = slots[1, f].astype(F32).reshape(64, F)
        ghn = gh * n64[:, cols]
        sums.append(jnp.sum(gh, axis=0, keepdims=True))
        sums_n.append(jnp.sum(ghn, axis=0, keepdims=True))
        one = 1.0 + scale_ref[:, cols]
        g64[:, cols] = gh * one
        m1 = m1 + jnp.sum(gh * one, axis=1, keepdims=True)
        m2 = m2 + jnp.sum(ghn * one, axis=1, keepdims=True)
    spread(jnp.concatenate(sums, axis=1), 1, 0, 0)
    spread(jnp.concatenate(sums_n, axis=1), 1, 1, 0)
    wa = vsum1(1, 1)
    vc = vsum3(0, 2, vb)
    wb = vsum2(1, 1, wa)
    m1 = m1 * (1.0 / D)
    m2 = m2 * (1.0 / D)
    for q in range(4):
        sl = slice(16 * q, 16 * q + 16)
        c64[sl, :] = (invs[q] * (g64[sl, :] - m1[sl] - n64[sl, :] * m2[sl])).astype(BF16)
    outs += [local(c64, corr_hbm, loc.at[9])]
    vd = vsum4(0, 2, vc)
    wc = vsum3(1, 1, wb)
    drain()
    vd.wait_recv()
    vec_ref[2] = vfin[0, 0, 0]
    vec_ref[3] = vfin[0, 0, 1]
    vec_ref[4] = vfin[0, 1, 0]
    wd = vsum4(1, 1, wc)
    for cp in outs:
        cp.wait()
    wd.wait_recv()
    vec_ref[0] = vfin[1, 0, 0]
    vec_ref[1] = vfin[1, 1, 0]
    drain()


def finish_kernel(
    rows_ref,
    grads_ref,
    act_ref,
    gp_ref,
    tok_ref,
    og_ref,
    gate_ref,
    table_ref,
    mixrows_ref,
    corr_ref,
    vec_ref,
    up_ref,
    down_ref,
    block_ref,
    tgrad_ref,
    shift_ref,
    scale_ref,
    ggrad_ref,
    router_ref,
):
    up_ref[0] = dot(rows_ref[...], gp_ref[...], 0, 0).astype(BF16)
    down_ref[0] = dot(act_ref[...], grads_ref[...], 0, 0).astype(BF16)
    block_ref[...] = (
        tok_ref[...].astype(F32) + gate_ref[...] * dot(table_ref[...], mixrows_ref[...], 1, 0)
    ).astype(BF16)
    tgrad_ref[...] = (
        og_ref[...].astype(F32) + dot(table_ref[...], corr_ref[...], 1, 0)
    ).astype(BF16)

    @pl.when(pl.program_id(0) == 0)
    def _():
        for i in range(D // TILE):
            cols = slice(i * TILE, i * TILE + TILE)
            shift_ref[:, cols] = vec_ref[0, i : i + 1, :]
            scale_ref[:, cols] = vec_ref[1, i : i + 1, :]
            ggrad_ref[:, cols] = vec_ref[2, i : i + 1, :]
            router_ref[0:1, cols] = vec_ref[3, i : i + 1, :]
            router_ref[1:2, cols] = vec_ref[4, i : i + 1, :]


def per_device(tokens, shift, scale, gate, router, up, down, picks, out_grad):
    hbm = pl.BlockSpec(memory_space=pl.ANY)
    vmem = pl.BlockSpec(memory_space=pltpu.VMEM)
    dma = pltpu.SemaphoreType.DMA
    shape = jax.ShapeDtypeStruct
    rows, grads, act, gp, mixrows, corr, table, vec = pl.pallas_call(
        exchange_kernel,
        out_shape=(
            shape((SLOTS, D), BF16),
            shape((SLOTS, D), BF16),
            shape((SLOTS, HU), BF16),
            shape((SLOTS, HU), BF16),
            shape((64, D), BF16),
            shape((64, D), BF16),
            shape((TOK, 64), BF16),
            shape((5, 8, TILE), F32),
        ),
        in_specs=[hbm, hbm, vmem, vmem, vmem, vmem, hbm, hbm, vmem],
        out_specs=(hbm, hbm, hbm, hbm, hbm, hbm, vmem, vmem),
        scratch_shapes=[
            pltpu.VMEM((TOK, D), BF16),
            pltpu.VMEM((TOK, D), BF16),
            pltpu.VMEM((D, HU), BF16),
            pltpu.VMEM((HU, D), BF16),
            pltpu.VMEM((2, NF, 2, MOST, F), BF16),
            pltpu.VMEM((2, NF, 2, 4, 4, MOST, F), BF16),
            pltpu.VMEM((2, NF // 2, 4, 2, MOST, F), BF16),
            pltpu.VMEM((2, SLOTS, D), BF16),
            pltpu.VMEM((SLOTS, HU), F32),
            pltpu.VMEM((SLOTS, HU), F32),
            pltpu.VMEM((SLOTS, HU), BF16),
            pltpu.VMEM((SLOTS, HU), BF16),
            pltpu.VMEM((2, NF, 2, 4, 4, MOST, F), BF16),
            pltpu.VMEM((2, NF, 4, 4, MOST, F), BF16),
            pltpu.VMEM((2, NF, 3, 4, MOST, F), BF16),
            pltpu.VMEM((2, NF, 8, MOST, F), BF16),
            pltpu.VMEM((2, NF, 3, 2, MOST, F), BF16),
            pltpu.VMEM((2, MOST, F), F32),
            pltpu.VMEM((2, NF, 4, 2, MOST, F), BF16),
            pltpu.VMEM((4, 2 * MOST, TOK), BF16),
            pltpu.VMEM((2 * MOST, D), F32),
            pltpu.VMEM((2 * MOST, D), BF16),
            pltpu.VMEM((64, D), F32),
            pltpu.VMEM((64, D), BF16),
            pltpu.VMEM((64, D), F32),
            pltpu.VMEM((64, D), BF16),
            pltpu.VMEM((64, D), BF16),
            pltpu.VMEM((2, 2, 2, 8, TILE), F32),
            pltpu.VMEM((2, 2, 8, TILE), F32),
            pltpu.VMEM((2, 4, 2, 8, TILE), F32),
            pltpu.VMEM((2, 4, 2, 8, TILE), F32),
            pltpu.VMEM((2, 2, 2, 8, TILE), F32),
            dma((10,)),
            dma((3,)),
            dma((3,)),
            dma((2, NF, 3)),
            dma((2, NF, 3)),
            dma((2, NF, 3)),
            dma((2, NF, 3)),
            dma((2, NF)),
            dma((2, NF)),
            dma((2, NF)),
            dma((2, NF)),
            dma((2, NF, 3)),
            dma((2, NF, 3)),
            dma((2, NF, 3)),
            dma((2, NF, 3)),
            dma((2, NF, 3)),
            dma((2, NF, 3)),
            dma((2, 8)),
            dma((2, 8)),
        ],
        compiler_params=pltpu.CompilerParams(
            collective_id=0, has_side_effects=True, vmem_limit_bytes=56 * 2**20
        ),
        cost_estimate=pl.CostEstimate(
            flops=12 * SLOTS * D * HU, bytes_accessed=24 * 2**20, transcendentals=SLOTS * HU
        ),
    )(
        tokens,
        out_grad,
        shift.reshape(1, D),
        scale.reshape(1, D),
        gate.reshape(1, D),
        router[0].T,
        up,
        down,
        picks[0],
    )
    steps = D // TILE
    one = lambda i: (0, 0)
    col = lambda i: (0, i)
    vecs = pl.BlockSpec((1, D), one)
    up_grad, down_grad, block, tgrad, shift_g, scale_g, gate_g, router_g = pl.pallas_call(
        finish_kernel,
        grid=(steps,),
        out_shape=(
            shape((1, D, HU), BF16),
            shape((1, HU, D), BF16),
            shape((TOK, D), BF16),
            shape((TOK, D), BF16),
            shape((1, D), F32),
            shape((1, D), F32),
            shape((1, D), F32),
            shape((2, D), F32),
        ),
        in_specs=[
            pl.BlockSpec((SLOTS, TILE), col),
            pl.BlockSpec((SLOTS, TILE), col),
            pl.BlockSpec((SLOTS, HU), one),
            pl.BlockSpec((SLOTS, HU), one),
            pl.BlockSpec((TOK, TILE), col),
            pl.BlockSpec((TOK, TILE), col),
            pl.BlockSpec((1, TILE), col),
            pl.BlockSpec((TOK, 64), one),
            pl.BlockSpec((64, TILE), col),
            pl.BlockSpec((64, TILE), col),
            pl.BlockSpec((5, 8, TILE), lambda i: (0, 0, 0)),
        ],
        out_specs=(
            pl.BlockSpec((1, TILE, HU), lambda i: (0, i, 0)),
            pl.BlockSpec((1, HU, TILE), lambda i: (0, 0, i)),
            pl.BlockSpec((TOK, TILE), col),
            pl.BlockSpec((TOK, TILE), col),
            vecs,
            vecs,
            vecs,
            pl.BlockSpec((2, D), one),
        ),
        cost_estimate=pl.CostEstimate(
            flops=4 * SLOTS * D * HU, bytes_accessed=18 * 2**20, transcendentals=0
        ),
    )(rows, grads, act, gp, tokens, out_grad, gate.reshape(1, D), table, mixrows, corr, vec)
    return (
        block,
        tgrad,
        up_grad,
        down_grad,
        router_g.T[None],
        shift_g[0],
        scale_g[0],
        gate_g[0],
    )


def solution(mesh):
    in_specs = (
        P("ctx", None),
        P(),
        P(),
        P(),
        P("exp", None, None),
        P("exp", None, "ctx"),
        P("exp", "ctx", None),
        P("exp", None, None),
        P("ctx", None),
    )
    out_specs = (
        P("ctx", None),
        P("ctx", None),
        P("exp", None, "ctx"),
        P("exp", "ctx", None),
        P("exp", None, None),
        P(),
        P(),
        P(),
    )
    return jax.shard_map(
        per_device, mesh=mesh, in_specs=in_specs, out_specs=out_specs, check_vma=False
    )
```

```python
import jax
import jax.numpy as jnp
from jax import lax
from jax.experimental import pallas as pl
from jax.experimental.pallas import tpu as pltpu
from jax.sharding import PartitionSpec as P

GELU_C = 0.7978845608028654
MESH = pl.DeviceIdType.MESH
F32 = jnp.float32
BF16 = jnp.bfloat16

D = 4096
HU = 512
TOK = 128
MOST = 8
NF = 4
F = D // NF
TILE = 512
STEP = 1024
SLOTS = 32 * MOST


def dot(a, b, ca, cb):
    return lax.dot_general(a, b, (((ca,), (cb,)), ((), ())), preferred_element_type=F32)


def exchange_kernel(
    tok_hbm,
    og_hbm,
    shift_ref,
    scale_ref,
    gate_ref,
    router_ref,
    up_hbm,
    down_hbm,
    picks_ref,
    rowmat0,
    rowmat1,
    act,
    gpre,
    x64,
    c64,
    tok,
    og,
    table_ref,
    vec_ref,
    up,
    down,
    own,
    got,
    relay,
    pre,
    gact,
    part,
    swap,
    first,
    mid,
    second,
    fin,
    slots,
    tables,
    mix,
    hid16,
    n64,
    og64,
    g64,
    n16,
    vsrc,
    vy,
    vx,
    vw,
    vz,
    loc,
    tab_s,
    tab_r,
    a1s,
    a1r,
    a2s,
    a2r,
    acs,
    acr,
    bcs,
    bcr,
    b1s,
    b1r,
    b2s,
    b2r,
    xs,
    xr,
    vs,
    vr,
    ws,
    wr,
):
    me = lax.axis_index("ctx")
    x = lax.axis_index("exp")
    z, y, c = me // 8, (me // 2) % 4, me % 2
    oc = 1 - c
    j = z // 2
    jo = 1 - j
    mate = (1 - z % 2) * 2

    def dev(zz, yy, cc, xx):
        return ((zz * 4 + yy) * 2 + cc, xx)

    def nxt(v, k):
        return (v + k) % 4

    pending = []

    def send(src, dst, ss, rs, to):
        cp = pltpu.make_async_remote_copy(
            src_ref=src, dst_ref=dst, send_sem=ss, recv_sem=rs, device_id=to, device_id_type=MESH
        )
        cp.start()
        pending.append(cp)
        return cp

    def local(src, dst, sem):
        cp = pltpu.make_async_copy(src, dst, sem)
        cp.start()
        return cp

    in_tok = local(tok_hbm, tok, loc.at[0])
    in_og = local(og_hbm, og, loc.at[1])

    bar = pltpu.get_barrier_semaphore()
    pl.semaphore_signal(bar, inc=1, device_id=dev(z, y, oc, x), device_id_type=MESH)
    for k in range(1, 4):
        pl.semaphore_signal(bar, inc=1, device_id=dev(nxt(z, k), y, c, x), device_id_type=MESH)
        pl.semaphore_signal(bar, inc=1, device_id=dev(z, nxt(y, k), c, x), device_id_type=MESH)
        pl.semaphore_signal(bar, inc=1, device_id=dev(nxt(z, k), y, oc, x), device_id_type=MESH)
        pl.semaphore_signal(bar, inc=1, device_id=dev(z, nxt(y, k), oc, x), device_id_type=MESH)
        pl.semaphore_signal(bar, inc=1, device_id=(me, nxt(x, k)), device_id_type=MESH)
        pl.semaphore_signal(bar, inc=1, device_id=dev(z, y, oc, nxt(x, k)), device_id_type=MESH)

    lanes = lax.broadcasted_iota(jnp.int32, (MOST, TOK), 1)
    subl = lax.broadcasted_iota(jnp.int32, (MOST, TOK), 0)
    tri = (
        lax.broadcasted_iota(jnp.int32, (TOK, TOK), 0) <= lax.broadcasted_iota(jnp.int32, (TOK, TOK), 1)
    ).astype(F32).astype(BF16)
    tabs = []
    for jj in range(2):
        ids = jnp.broadcast_to(picks_ref[jj : jj + 1, :], (MOST, TOK)) - me * TOK
        inside = (ids >= 0) & (ids < TOK)
        inside_f = jnp.where(inside, 1.0, 0.0)
        count = dot(inside_f.astype(BF16), tri, 1, 0)
        hit = jnp.where(inside & (count == (subl + 1).astype(F32)), 1.0, 0.0)
        where_tok = jnp.sum(hit * ids.astype(F32), axis=1, keepdims=True)
        there = jnp.sum(hit, axis=1, keepdims=True)
        tabs.append(jnp.where((where_tok == lanes.astype(F32)) & (there > 0.5), 1.0, 0.0))
    table = jnp.concatenate(tabs, axis=0).astype(BF16)
    tables[x] = table

    in_tok.wait()
    trow = dot(table, tok[...], 1, 0)
    cen = trow - jnp.mean(trow, axis=1, keepdims=True)
    inv = lax.rsqrt(jnp.mean(cen * cen, axis=1, keepdims=True) + 1e-06)
    row_there = jnp.sum(table.astype(F32), axis=1, keepdims=True)
    n16[...] = cen * inv
    hid = ((cen * inv * (1.0 + scale_ref[...]) + shift_ref[...]) * row_there).astype(BF16)
    hid16[...] = hid
    hidf = hid.astype(F32)
    rout = router_ref[...].astype(F32)
    logits = jnp.concatenate(
        [
            jnp.sum(hidf[MOST * jj : MOST * jj + MOST] * rout[jj : jj + 1], axis=1, keepdims=True)
            for jj in range(2)
        ],
        axis=0,
    )
    weight = 1.0 / (1.0 + jnp.exp(-logits))
    for f in range(NF):
        for jj in range(2):
            own[0, f, jj] = hidf[MOST * jj : MOST * jj + MOST, f * F : f * F + F].astype(BF16)
    pl.semaphore_wait(bar, 19)

    tabc = [
        send(tables.at[x], tables.at[x], tab_s.at[k - 1], tab_r.at[k - 1], (me, nxt(x, k)))
        for k in range(1, 4)
    ]

    def recv(cps):
        for cp in cps:
            cp.wait_recv()

    def zfirst(f):
        return f % 2 == 0

    def gather1(a, f):
        if zfirst(f):
            return [
                send(
                    own.at[a, f, nxt(z, k) // 2],
                    got.at[a, f, c, y, z],
                    a1s.at[a, f, k - 1],
                    a1r.at[a, f, k - 1],
                    dev(nxt(z, k), y, c, x),
                )
                for k in range(1, 4)
            ]
        return [
            send(
                own.at[a, f],
                relay.at[a, f // 2, y],
                a1s.at[a, f, k - 1],
                a1r.at[a, f, k - 1],
                dev(z, nxt(y, k), c, x),
            )
            for k in range(1, 4)
        ]

    def gather2(a, f, g1):
        if zfirst(f):
            got[a, f, c, y, z] = own[a, f, j]
            recv(g1)
            return [
                send(
                    got.at[a, f, c, y],
                    got.at[a, f, c, y],
                    a2s.at[a, f, k - 1],
                    a2r.at[a, f, k - 1],
                    dev(z, nxt(y, k), c, x),
                )
                for k in range(1, 4)
            ]
        relay[a, f // 2, y] = own[a, f]
        recv(g1)
        cps = [
            send(
                relay.at[a, f // 2, :, nxt(z, k) // 2],
                got.at[a, f, c, :, z],
                a2s.at[a, f, k - 1],
                a2r.at[a, f, k - 1],
                dev(nxt(z, k), y, c, x),
            )
            for k in range(1, 4)
        ]
        got[a, f, c, :, z] = relay[a, f // 2, :, j]
        return cps

    def gather3(a, f, g2):
        recv(g2)
        return send(
            got.at[a, f, c], got.at[a, f, c], acs.at[a, f], acr.at[a, f], dev(z, y, oc, x)
        )

    def rows_ready(a, f, g3):
        g3.wait_recv()

        def pair(i, _):
            cc, yy, zz = i // 8, (i // 2) % 4, (i % 2) * 2
            two = got[a, f, cc, yy, pl.ds(zz, 2)].astype(F32).reshape(16, F)
            (rowmat1 if a else rowmat0)[pl.ds(pl.multiple_of(i * 16, 16), 16), f * F : f * F + F] = two.astype(BF16)
            return 0

        lax.fori_loop(0, 16, pair, 0)

    def partial(a, f):
        left = (act if a == 0 else gpre)[...]
        for t in range(F // TILE):
            lo = f * F + t * TILE
            if a == 0:
                prod = dot(left, down[:, lo : lo + TILE], 1, 0)
            else:
                prod = dot(left, up[lo : lo + TILE, :], 1, 1)
            part[a, f, :, :, :, :, t * TILE : t * TILE + TILE] = prod.reshape(
                2, 4, 4, MOST, TILE
            ).astype(BF16)
        return send(part.at[a, f, oc], swap.at[a, f], bcs.at[a, f], bcr.at[a, f], dev(z, y, oc, x))

    def return1(a, f, cp):
        cp.wait_recv()

        def add(i, _):
            yy, zz = i // 4, i % 4
            swap[a, f, yy, zz] = (
                swap[a, f, yy, zz].astype(F32) + part[a, f, c, yy, zz].astype(F32)
            ).astype(BF16)
            return 0

        lax.fori_loop(0, 16, add, 0)
        if zfirst(f):
            return [
                send(
                    swap.at[a, f, nxt(y, k)],
                    first.at[a, f, k - 1],
                    b1s.at[a, f, k - 1],
                    b1r.at[a, f, k - 1],
                    dev(z, nxt(y, k), c, x),
                )
                for k in range(1, 4)
            ]
        return [
            send(
                swap.at[a, f, :, nxt(z, k)],
                first.at[a, f, k - 1],
                b1s.at[a, f, k - 1],
                b1r.at[a, f, k - 1],
                dev(nxt(z, k), y, c, x),
            )
            for k in range(1, 4)
        ]

    def return2(a, f, cps):
        recv(cps)
        if zfirst(f):

            def add(i, _):
                mid[a, f, i] = (
                    swap[a, f, y, i].astype(F32)
                    + first[a, f, 0, i].astype(F32)
                    + first[a, f, 1, i].astype(F32)
                    + first[a, f, 2, i].astype(F32)
                ).astype(BF16)
                return 0

            lax.fori_loop(0, 4, add, 0)
            return [
                send(
                    mid.at[a, f, nxt(z, k)],
                    second.at[a, f, k - 1, 0],
                    b2s.at[a, f, k - 1],
                    b2r.at[a, f, k - 1],
                    dev(nxt(z, k), y, c, x),
                )
                for k in range(1, 4)
            ]

        def add(i, _):
            mid[a, f, 2 * i + j] = (
                swap[a, f, i, z].astype(F32) + first[a, f, mate, i].astype(F32)
            ).astype(BF16)
            mid[a, f, 2 * i + jo] = (
                first[a, f, 1, i].astype(F32) + first[a, f, 2 - mate, i].astype(F32)
            ).astype(BF16)
            return 0

        lax.fori_loop(0, 4, add, 0)
        return [
            send(
                mid.at[a, f, pl.ds(2 * nxt(y, k), 2)],
                second.at[a, f, k - 1],
                b2s.at[a, f, k - 1],
                b2r.at[a, f, k - 1],
                dev(z, nxt(y, k), c, x),
            )
            for k in range(1, 4)
        ]

    def return3(a, f, cps):
        recv(cps)
        if zfirst(f):
            fin[j] = mid[a, f, z].astype(F32) + second[a, f, mate, 0].astype(F32)
            fin[jo] = second[a, f, 1, 0].astype(F32) + second[a, f, 2 - mate, 0].astype(F32)
        else:
            fin[...] = (
                mid[a, f, pl.ds(2 * y, 2)].astype(F32)
                + second[a, f, 0].astype(F32)
                + second[a, f, 1].astype(F32)
                + second[a, f, 2].astype(F32)
            )
        return fin[...].reshape(2 * MOST, F)

    def to_x(a, f, rows):
        slots[a, f, x] = rows.reshape(2, MOST, F).astype(BF16)
        return [
            send(
                slots.at[a, f, x],
                slots.at[a, f, x],
                xs.at[a, f, k - 1],
                xr.at[a, f, k - 1],
                (me, nxt(x, k)),
            )
            for k in range(1, 4)
        ]

    def spread(row, stage, cc, n):
        for i in range(D // TILE):
            vsrc[stage, cc, n, i : i + 1, :] = row[:, i * TILE : i * TILE + TILE]

    def vsum1(s, n):
        cut = pl.ds(0, n)
        cps = []
        for i in range(1, 8):
            k, cc = i // 2, (c if i % 2 == 0 else oc)
            cps.append(
                send(
                    vsrc.at[s, cc, cut],
                    vy.at[2 * y + c, cut],
                    vs.at[0, i - 1],
                    vr.at[0, i - 1],
                    dev(z, nxt(y, k), cc, x),
                )
            )
        vy[2 * y + c, cut] = vsrc[s, c, cut]
        return cps

    def vsum2(s, n, cps):
        recv(cps)
        cut = pl.ds(0, n)
        if s == 0:
            total = vy[0, cut]
            for i in range(1, 8):
                total = total + vy[i, cut]
        else:
            total = ((vw[0] + vw[1]) + (vw[2] + vw[3]))[None]
        vz[s, z, c, cut] = total
        cps = []
        for i in range(1, 8):
            k, cc = i // 2, (c if i % 2 == 0 else oc)
            cps.append(
                send(
                    vz.at[s, z, c, cut],
                    vz.at[s, z, c, cut],
                    vs.at[1 + s, i - 1],
                    vr.at[1 + s, i - 1],
                    dev(nxt(z, k), y, cc, x),
                )
            )
        return cps

    def vsum3(s, cps, where):
        recv(cps)
        for cc, n, out in where:
            vec_ref[out] = (vz[s, 0, cc, n] + vz[s, 1, cc, n]) + (vz[s, 2, cc, n] + vz[s, 3, cc, n])

    def xsum1():
        cps = []
        for i in range(1, 8):
            k, cc = i // 2, (c if i % 2 == 0 else oc)
            cps.append(
                send(
                    vsrc.at[1, cc, 0],
                    vx.at[2 * x + c],
                    ws.at[i - 1],
                    wr.at[i - 1],
                    dev(z, y, cc, nxt(x, k)),
                )
            )
        vx[2 * x + c] = vsrc[1, c, 0]
        return cps

    def xsum2(cps):
        recv(cps)
        total = vx[0]
        for i in range(1, 8):
            total = total + vx[i]
        vw[y] = total
        return [
            send(vw.at[y], vw.at[y], ws.at[6 + k], wr.at[6 + k], dev(z, nxt(y, k), c, x))
            for k in range(1, 4)
        ]

    drained = [0]

    def drain():
        for cp in pending[drained[0] :]:
            cp.wait_send()
        drained[0] = len(pending)

    parts = range(NF)
    pairs = [(f, f + 1) for f in range(0, NF, 2)]
    last = len(pairs) - 1
    g1, g2, g3 = {}, {}, {}
    r0, r1, r2, r3 = {}, {}, {}, {}

    def each(step, a, p, into, *before):
        for f in pairs[p]:
            into[a, f] = step(a, f, *[b[a, f] for b in before])

    for p in range(last + 1):
        each(gather1, 0, p, g1)
    in_og.wait()
    mixv = dot(table, og[...], 1, 0) * gate_ref[...]
    mix[...] = mixv
    gradv = weight * mixv
    for f in range(NF):
        for jj in range(2):
            own[1, f, jj] = gradv[MOST * jj : MOST * jj + MOST, f * F : f * F + F].astype(BF16)
    in_up = local(up_hbm.at[0], up, loc.at[2])
    in_down = local(down_hbm.at[0], down, loc.at[3])
    each(gather1, 1, 0, g1)
    for p in range(last + 1):
        each(gather2, 0, p, g2, g1)
    for p in range(1, last + 1):
        each(gather1, 1, p, g1)

    recv(tabc)
    tabt = tables[...].astype(F32).reshape(64, TOK).T.astype(BF16)
    table_ref[...] = tabt
    invs = []

    def slot_rows(q):
        sl = slice(16 * q, 16 * q + 16)
        t16 = dot(tables[q], tok[...], 1, 0)
        c16 = t16 - jnp.mean(t16, axis=1, keepdims=True)
        i16 = lax.rsqrt(jnp.mean(c16 * c16, axis=1, keepdims=True) + 1e-06)
        invs.append(i16)
        n64[sl, :] = c16 * i16
        og64[sl, :] = dot(tables[q], og[...], 1, 0).astype(BF16)

    slot_rows(0)
    each(gather2, 1, 0, g2, g1)
    for q in range(1, 4):
        slot_rows(q)
    for p in range(last + 1):
        each(gather3, 0, p, g3, g2)
        if p > 0:
            each(gather2, 1, p, g2, g1)
    in_up.wait()
    for f in parts:
        rows_ready(0, f, g3[0, f])
        acc = dot(rowmat0[:, f * F : f * F + F], up[f * F : f * F + F, :], 1, 0)
        pre[...] = acc if f == 0 else pre[...] + acc
    prev = pre[...]
    tang = jnp.tanh(GELU_C * (prev + 0.044715 * prev * prev * prev))
    act[...] = (0.5 * prev * (1.0 + tang)).astype(BF16)
    pre[...] = 0.5 * (1.0 + tang) + 0.5 * prev * (1.0 - tang * tang) * GELU_C * (
        1.0 + 3.0 * 0.044715 * prev * prev
    )
    in_down.wait()
    for p in range(last + 1):
        each(partial, 0, p, r0)
    each(gather3, 1, 0, g3, g2)
    for p in range(last + 1):
        each(return1, 0, p, r1, r0)
    for p in range(last + 1):
        if p > 0:
            each(gather3, 1, p, g3, g2)
        for f in pairs[p]:
            rows_ready(1, f, g3[1, f])
            acc = dot(rowmat1[:, f * F : f * F + F], down[:, f * F : f * F + F], 1, 1)
            gact[...] = acc if f == 0 else gact[...] + acc
    gpre[...] = (gact[...] * pre[...]).astype(BF16)
    for p in range(last + 1):
        each(partial, 1, p, r0)
    for p in range(last + 1):
        each(return2, 0, p, r2, r1)
        each(return1, 1, p, r1, r0)
    grad_w = jnp.zeros((2 * MOST, 1), F32)
    for p in range(last + 1):
        for f in pairs[p]:
            rows = return3(0, f, r2[0, f])
            grad_w = grad_w + jnp.sum(rows * mix[:, f * F : f * F + F], axis=1, keepdims=True)
            r3[0, f] = to_x(0, f, rows * weight)
        if p < last:
            each(return2, 1, p, r2, r1)
    grad_logit = grad_w * weight * (1.0 - weight)
    hg = hid16[...].astype(F32) * grad_logit
    spread(jnp.sum(hg[:MOST], axis=0, keepdims=True), 0, 0, 1)
    spread(jnp.sum(hg[MOST:], axis=0, keepdims=True), 0, 1, 0)
    vsrc[0, 1, 1] = jnp.zeros((8, TILE), F32)
    each(return2, 1, last, r2, r1)
    drain()
    sums1, sums2 = [], []

    def back_rows(f):
        rows = return3(1, f, r2[1, f])
        add = [
            grad_logit[MOST * jj : MOST * jj + MOST]
            * router_ref[jj : jj + 1, f * F : f * F + F].astype(F32)
            for jj in range(2)
        ]
        rows = rows + jnp.concatenate(add, axis=0)
        sums1.append(jnp.sum(rows, axis=0, keepdims=True))
        sums2.append(jnp.sum(rows * n16[:, f * F : f * F + F], axis=0, keepdims=True))
        return rows

    for p in range(last):
        for f in pairs[p]:
            r3[1, f] = to_x(1, f, back_rows(f))
    ends = [back_rows(f) for f in pairs[last]]
    spread(jnp.concatenate(sums1, axis=1), 1, 0, 0)
    spread(jnp.concatenate(sums2, axis=1), 1, 1, 0)
    wa = xsum1()
    for f, rows in zip(pairs[last], ends):
        r3[1, f] = to_x(1, f, rows)
    sums = []
    for f in parts:
        cols = slice(f * F, f * F + F)
        recv(r3[0, f])
        outrows = slots[0, f].astype(F32).reshape(64, F)
        sums.append(jnp.sum(outrows * og64[:, cols].astype(F32), axis=0, keepdims=True))
        x64[:, cols] = outrows.astype(BF16)
    spread(jnp.concatenate(sums, axis=1), 0, 0, 0)
    va = vsum1(0, 2)
    wb = xsum2(wa)
    vb = vsum2(0, 2, va)
    wc = vsum2(1, 1, wb)
    m1 = jnp.zeros((64, 1), F32)
    m2 = jnp.zeros((64, 1), F32)
    for f in parts:
        cols = slice(f * F, f * F + F)
        recv(r3[1, f])
        gh = slots[1, f].astype(F32).reshape(64, F)
        ghn = gh * n64[:, cols]
        one = 1.0 + scale_ref[:, cols]
        g64[:, cols] = gh * one
        m1 = m1 + jnp.sum(gh * one, axis=1, keepdims=True)
        m2 = m2 + jnp.sum(ghn * one, axis=1, keepdims=True)
    m1 = m1 * (1.0 / D)
    m2 = m2 * (1.0 / D)
    for q in range(4):
        sl = slice(16 * q, 16 * q + 16)
        c64[sl, :] = (invs[q] * (g64[sl, :] - m1[sl] - n64[sl, :] * m2[sl])).astype(BF16)
    vsum3(0, vb, [(0, 0, 2), (0, 1, 3), (1, 0, 4)])
    drain()
    vsum3(1, wc, [(0, 0, 0), (1, 0, 1)])


def finish_kernel(
    rows,
    grads,
    act,
    gp,
    mixrows,
    corr,
    tok,
    og,
    table_ref,
    vec_ref,
    gate_ref,
    up_hbm,
    down_hbm,
    block_hbm,
    tgrad_hbm,
    shift_ref,
    scale_ref,
    ggrad_ref,
    router_ref,
    up,
    down,
    block,
    tgrad,
    act_t,
    sem_out,
):
    steps = D // STEP
    for i in range(D // TILE):
        cols = slice(i * TILE, i * TILE + TILE)
        shift_ref[:, cols] = vec_ref[0, i : i + 1, :]
        scale_ref[:, cols] = vec_ref[1, i : i + 1, :]
        ggrad_ref[:, cols] = vec_ref[2, i : i + 1, :]
        router_ref[0:1, cols] = vec_ref[3, i : i + 1, :]
        router_ref[1:2, cols] = vec_ref[4, i : i + 1, :]
    act_t[...] = act[...].astype(F32).T.astype(BF16)
    stores = []

    def store(src, dst, sem):
        cp = pltpu.make_async_copy(src, dst, sem)
        cp.start()
        stores.append(cp)

    for t in range(steps):
        cols = pl.ds(t * STEP, STEP)
        up[cols, :] = dot(rows[:, cols], gp[...], 0, 0).astype(BF16)
        store(up.at[cols], up_hbm.at[0, cols], sem_out.at[t, 0])
        down[:, cols] = dot(act_t[...], grads[:, cols], 1, 0).astype(BF16)
        store(down.at[:, cols], down_hbm.at[0, :, cols], sem_out.at[t, 1])
        block[:, cols] = (
            tok[:, cols].astype(F32)
            + gate_ref[:, cols] * dot(table_ref[...], mixrows[:, cols], 1, 0)
        ).astype(BF16)
        store(block.at[:, cols], block_hbm.at[:, cols], sem_out.at[t, 2])
        tgrad[:, cols] = (
            og[:, cols].astype(F32) + dot(table_ref[...], corr[:, cols], 1, 0)
        ).astype(BF16)
        store(tgrad.at[:, cols], tgrad_hbm.at[:, cols], sem_out.at[t, 3])
    for cp in stores:
        cp.wait()


def per_device(tokens, shift, scale, gate, router, up, down, picks, out_grad):
    hbm = pl.BlockSpec(memory_space=pl.ANY)
    vmem = pl.BlockSpec(memory_space=pltpu.VMEM)
    dma = pltpu.SemaphoreType.DMA
    shape = jax.ShapeDtypeStruct
    vm = pltpu.VMEM
    *kept, table, vec = pl.pallas_call(
        exchange_kernel,
        out_shape=(
            vm((SLOTS, D), BF16),
            vm((SLOTS, D), BF16),
            vm((SLOTS, HU), BF16),
            vm((SLOTS, HU), BF16),
            vm((64, D), BF16),
            vm((64, D), BF16),
            vm((TOK, D), BF16),
            vm((TOK, D), BF16),
            vm((TOK, 64), BF16),
            vm((5, 8, TILE), F32),
        ),
        in_specs=[hbm, hbm, vmem, vmem, vmem, vmem, hbm, hbm, vmem],
        out_specs=(vmem,) * 10,
        scratch_shapes=[
            pltpu.VMEM((D, HU), BF16),
            pltpu.VMEM((HU, D), BF16),
            pltpu.VMEM((2, NF, 2, MOST, F), BF16),
            pltpu.VMEM((2, NF, 2, 4, 4, MOST, F), BF16),
            pltpu.VMEM((2, NF // 2, 4, 2, MOST, F), BF16),
            pltpu.VMEM((SLOTS, HU), F32),
            pltpu.VMEM((SLOTS, HU), F32),
            pltpu.VMEM((2, NF, 2, 4, 4, MOST, F), BF16),
            pltpu.VMEM((2, NF, 4, 4, MOST, F), BF16),
            pltpu.VMEM((2, NF, 3, 4, MOST, F), BF16),
            pltpu.VMEM((2, NF, 8, MOST, F), BF16),
            pltpu.VMEM((2, NF, 3, 2, MOST, F), BF16),
            pltpu.VMEM((2, MOST, F), F32),
            pltpu.VMEM((2, NF, 4, 2, MOST, F), BF16),
            pltpu.VMEM((4, 2 * MOST, TOK), BF16),
            pltpu.VMEM((2 * MOST, D), F32),
            pltpu.VMEM((2 * MOST, D), BF16),
            pltpu.VMEM((64, D), F32),
            pltpu.VMEM((64, D), BF16),
            pltpu.VMEM((64, D), F32),
            pltpu.VMEM((2 * MOST, D), F32),
            pltpu.VMEM((2, 2, 2, 8, TILE), F32),
            pltpu.VMEM((8, 2, 8, TILE), F32),
            pltpu.VMEM((8, 8, TILE), F32),
            pltpu.VMEM((4, 8, TILE), F32),
            pltpu.VMEM((2, 4, 2, 2, 8, TILE), F32),
            dma((4,)),
            dma((3,)),
            dma((3,)),
            dma((2, NF, 3)),
            dma((2, NF, 3)),
            dma((2, NF, 3)),
            dma((2, NF, 3)),
            dma((2, NF)),
            dma((2, NF)),
            dma((2, NF)),
            dma((2, NF)),
            dma((2, NF, 3)),
            dma((2, NF, 3)),
            dma((2, NF, 3)),
            dma((2, NF, 3)),
            dma((2, NF, 3)),
            dma((2, NF, 3)),
            dma((3, 7)),
            dma((3, 7)),
            dma((10,)),
            dma((10,)),
        ],
        compiler_params=pltpu.CompilerParams(
            collective_id=0, has_side_effects=True, vmem_limit_bytes=55 * 2**20
        ),
        cost_estimate=pl.CostEstimate(
            flops=12 * SLOTS * D * HU, bytes_accessed=24 * 2**20, transcendentals=SLOTS * HU
        ),
    )(
        tokens,
        out_grad,
        shift.reshape(1, D),
        scale.reshape(1, D),
        gate.reshape(1, D),
        router[0].T,
        up,
        down,
        picks[0],
    )
    kept = [pltpu.with_memory_space_constraint(a, vm) for a in (*kept, table, vec)]
    up_grad, down_grad, block, tgrad, shift_g, scale_g, gate_g, router_g = pl.pallas_call(
        finish_kernel,
        out_shape=(
            shape((1, D, HU), BF16),
            shape((1, HU, D), BF16),
            shape((TOK, D), BF16),
            shape((TOK, D), BF16),
            shape((1, D), F32),
            shape((1, D), F32),
            shape((1, D), F32),
            shape((2, D), F32),
        ),
        in_specs=[vmem] * 11,
        out_specs=(hbm, hbm, hbm, hbm, vmem, vmem, vmem, vmem),
        scratch_shapes=[
            vm((D, HU), BF16),
            vm((HU, D), BF16),
            vm((TOK, D), BF16),
            vm((TOK, D), BF16),
            vm((HU, SLOTS), BF16),
            dma((D // STEP, 4)),
        ],
        compiler_params=pltpu.CompilerParams(vmem_limit_bytes=44 * 2**20),
        cost_estimate=pl.CostEstimate(
            flops=4 * SLOTS * D * HU, bytes_accessed=10 * 2**20, transcendentals=0
        ),
    )(*kept, gate.reshape(1, D))
    return (
        block,
        tgrad,
        up_grad,
        down_grad,
        router_g.T[None],
        shift_g[0],
        scale_g[0],
        gate_g[0],
    )


def solution(mesh):
    in_specs = (
        P("ctx", None),
        P(),
        P(),
        P(),
        P("exp", None, None),
        P("exp", None, "ctx"),
        P("exp", "ctx", None),
        P("exp", None, None),
        P("ctx", None),
    )
    out_specs = (
        P("ctx", None),
        P("ctx", None),
        P("exp", None, "ctx"),
        P("exp", "ctx", None),
        P("exp", None, None),
        P(),
        P(),
        P(),
    )
    return jax.shard_map(
        per_device, mesh=mesh, in_specs=in_specs, out_specs=out_specs, check_vma=False
    )
```

```python
import jax
import jax.numpy as jnp
from jax import lax
from jax.experimental import pallas as pl
from jax.experimental.pallas import tpu as pltpu
from jax.sharding import PartitionSpec as P

GELU_C = 0.7978845608028654
MESH = pl.DeviceIdType.MESH
F32 = jnp.float32
BF16 = jnp.bfloat16

D = 4096
HU = 512
TOK = 128
MOST = 8
NF = 4
F = D // NF
TILE = 512
STEP = 1024
SLOTS = 32 * MOST


def dot(a, b, ca, cb):
    return lax.dot_general(a, b, (((ca,), (cb,)), ((), ())), preferred_element_type=F32)


def exchange_kernel(
    tok_hbm,
    og_hbm,
    shift_ref,
    scale_ref,
    gate_ref,
    router_ref,
    up_hbm,
    down_hbm,
    picks_ref,
    rowmat0,
    rowmat1,
    act,
    gpre,
    x64,
    c64,
    tok,
    og,
    table_ref,
    vec_ref,
    up,
    down,
    own,
    got,
    relay,
    pre,
    gact,
    part,
    swap,
    first,
    mid,
    second,
    fin,
    slots,
    tables,
    mix,
    hid16,
    n64,
    og64,
    g64,
    n16,
    vsrc,
    vy,
    vx,
    vw,
    vz,
    loc,
    tab_s,
    tab_r,
    a1s,
    a1r,
    a2s,
    a2r,
    acs,
    acr,
    bcs,
    bcr,
    b1s,
    b1r,
    b2s,
    b2r,
    xs,
    xr,
    vs,
    vr,
    ws,
    wr,
):
    me = lax.axis_index("ctx")
    x = lax.axis_index("exp")
    z, y, c = me // 8, (me // 2) % 4, me % 2
    oc = 1 - c
    j = z // 2
    jo = 1 - j
    mate = (1 - z % 2) * 2

    def dev(zz, yy, cc, xx):
        return ((zz * 4 + yy) * 2 + cc, xx)

    def nxt(v, k):
        return (v + k) % 4

    pending = []

    def send(src, dst, ss, rs, to):
        cp = pltpu.make_async_remote_copy(
            src_ref=src, dst_ref=dst, send_sem=ss, recv_sem=rs, device_id=to, device_id_type=MESH
        )
        cp.start()
        pending.append(cp)
        return cp

    def local(src, dst, sem):
        cp = pltpu.make_async_copy(src, dst, sem)
        cp.start()
        return cp

    in_tok = local(tok_hbm, tok, loc.at[0])
    in_og = local(og_hbm, og, loc.at[1])

    bar = pltpu.get_barrier_semaphore()
    pl.semaphore_signal(bar, inc=1, device_id=dev(z, y, oc, x), device_id_type=MESH)
    for k in range(1, 4):
        pl.semaphore_signal(bar, inc=1, device_id=dev(nxt(z, k), y, c, x), device_id_type=MESH)
        pl.semaphore_signal(bar, inc=1, device_id=dev(z, nxt(y, k), c, x), device_id_type=MESH)
        pl.semaphore_signal(bar, inc=1, device_id=dev(nxt(z, k), y, oc, x), device_id_type=MESH)
        pl.semaphore_signal(bar, inc=1, device_id=dev(z, nxt(y, k), oc, x), device_id_type=MESH)
        pl.semaphore_signal(bar, inc=1, device_id=(me, nxt(x, k)), device_id_type=MESH)
        pl.semaphore_signal(bar, inc=1, device_id=dev(z, y, oc, nxt(x, k)), device_id_type=MESH)

    lanes = lax.broadcasted_iota(jnp.int32, (MOST, TOK), 1)
    subl = lax.broadcasted_iota(jnp.int32, (MOST, TOK), 0)
    tri = (
        lax.broadcasted_iota(jnp.int32, (TOK, TOK), 0) <= lax.broadcasted_iota(jnp.int32, (TOK, TOK), 1)
    ).astype(F32).astype(BF16)
    tabs = []
    for jj in range(2):
        ids = jnp.broadcast_to(picks_ref[jj : jj + 1, :], (MOST, TOK)) - me * TOK
        inside = (ids >= 0) & (ids < TOK)
        inside_f = jnp.where(inside, 1.0, 0.0)
        count = dot(inside_f.astype(BF16), tri, 1, 0)
        hit = jnp.where(inside & (count == (subl + 1).astype(F32)), 1.0, 0.0)
        where_tok = jnp.sum(hit * ids.astype(F32), axis=1, keepdims=True)
        there = jnp.sum(hit, axis=1, keepdims=True)
        tabs.append(jnp.where((where_tok == lanes.astype(F32)) & (there > 0.5), 1.0, 0.0))
    table = jnp.concatenate(tabs, axis=0).astype(BF16)
    tables[x] = table

    in_tok.wait()
    trow = dot(table, tok[...], 1, 0)
    cen = trow - jnp.mean(trow, axis=1, keepdims=True)
    inv = lax.rsqrt(jnp.mean(cen * cen, axis=1, keepdims=True) + 1e-06)
    row_there = jnp.sum(table.astype(F32), axis=1, keepdims=True)
    n16[...] = cen * inv
    hid = ((cen * inv * (1.0 + scale_ref[...]) + shift_ref[...]) * row_there).astype(BF16)
    hid16[...] = hid
    hidf = hid.astype(F32)
    rout = router_ref[...].astype(F32)
    logits = jnp.concatenate(
        [
            jnp.sum(hidf[MOST * jj : MOST * jj + MOST] * rout[jj : jj + 1], axis=1, keepdims=True)
            for jj in range(2)
        ],
        axis=0,
    )
    weight = 1.0 / (1.0 + jnp.exp(-logits))
    for f in range(NF):
        for jj in range(2):
            own[0, f, jj] = hidf[MOST * jj : MOST * jj + MOST, f * F : f * F + F].astype(BF16)
    pl.semaphore_wait(bar, 19)

    tabc = [
        send(tables.at[x], tables.at[x], tab_s.at[k - 1], tab_r.at[k - 1], (me, nxt(x, k)))
        for k in range(1, 4)
    ]

    def recv(cps):
        for cp in cps:
            cp.wait_recv()

    def zfirst(f):
        return f % 2 == 0

    def gather1(a, f):
        if zfirst(f):
            return [
                send(
                    own.at[a, f, nxt(z, k) // 2],
                    got.at[a, f, c, y, z],
                    a1s.at[a, f, k - 1],
                    a1r.at[a, f, k - 1],
                    dev(nxt(z, k), y, c, x),
                )
                for k in range(1, 4)
            ]
        return [
            send(
                own.at[a, f],
                relay.at[a, f // 2, y],
                a1s.at[a, f, k - 1],
                a1r.at[a, f, k - 1],
                dev(z, nxt(y, k), c, x),
            )
            for k in range(1, 4)
        ]

    def gather2(a, f, g1):
        if zfirst(f):
            got[a, f, c, y, z] = own[a, f, j]
            recv(g1)
            return [
                send(
                    got.at[a, f, c, y],
                    got.at[a, f, c, y],
                    a2s.at[a, f, k - 1],
                    a2r.at[a, f, k - 1],
                    dev(z, nxt(y, k), c, x),
                )
                for k in range(1, 4)
            ]
        relay[a, f // 2, y] = own[a, f]
        recv(g1)
        cps = [
            send(
                relay.at[a, f // 2, :, nxt(z, k) // 2],
                got.at[a, f, c, :, z],
                a2s.at[a, f, k - 1],
                a2r.at[a, f, k - 1],
                dev(nxt(z, k), y, c, x),
            )
            for k in range(1, 4)
        ]
        got[a, f, c, :, z] = relay[a, f // 2, :, j]
        return cps

    def gather3(a, f, g2):
        recv(g2)
        return send(
            got.at[a, f, c], got.at[a, f, c], acs.at[a, f], acr.at[a, f], dev(z, y, oc, x)
        )

    def rows_ready(a, f, g3):
        g3.wait_recv()

        def pair(i, _):
            cc, yy, zz = i // 8, (i // 2) % 4, (i % 2) * 2
            two = got[a, f, cc, yy, pl.ds(zz, 2)].astype(F32).reshape(16, F)
            (rowmat1 if a else rowmat0)[pl.ds(pl.multiple_of(i * 16, 16), 16), f * F : f * F + F] = two.astype(BF16)
            return 0

        lax.fori_loop(0, 16, pair, 0)

    def partial(a, f):
        left = (act if a == 0 else gpre)[...]
        for t in range(F // TILE):
            lo = f * F + t * TILE
            if a == 0:
                prod = dot(left, down[:, lo : lo + TILE], 1, 0)
            else:
                prod = dot(left, up[lo : lo + TILE, :], 1, 1)
            part[a, f, :, :, :, :, t * TILE : t * TILE + TILE] = prod.reshape(
                2, 4, 4, MOST, TILE
            ).astype(BF16)
        return send(part.at[a, f, oc], swap.at[a, f], bcs.at[a, f], bcr.at[a, f], dev(z, y, oc, x))

    def return1(a, f, cp):
        cp.wait_recv()

        def add(i, _):
            yy, zz = i // 4, i % 4
            swap[a, f, yy, zz] = (
                swap[a, f, yy, zz].astype(F32) + part[a, f, c, yy, zz].astype(F32)
            ).astype(BF16)
            return 0

        lax.fori_loop(0, 16, add, 0)
        if zfirst(f):
            return [
                send(
                    swap.at[a, f, nxt(y, k)],
                    first.at[a, f, k - 1],
                    b1s.at[a, f, k - 1],
                    b1r.at[a, f, k - 1],
                    dev(z, nxt(y, k), c, x),
                )
                for k in range(1, 4)
            ]
        return [
            send(
                swap.at[a, f, :, nxt(z, k)],
                first.at[a, f, k - 1],
                b1s.at[a, f, k - 1],
                b1r.at[a, f, k - 1],
                dev(nxt(z, k), y, c, x),
            )
            for k in range(1, 4)
        ]

    def return2(a, f, cps):
        recv(cps)
        if zfirst(f):

            def add(i, _):
                mid[a, f, i] = (
                    swap[a, f, y, i].astype(F32)
                    + first[a, f, 0, i].astype(F32)
                    + first[a, f, 1, i].astype(F32)
                    + first[a, f, 2, i].astype(F32)
                ).astype(BF16)
                return 0

            lax.fori_loop(0, 4, add, 0)
            return [
                send(
                    mid.at[a, f, nxt(z, k)],
                    second.at[a, f, k - 1, 0],
                    b2s.at[a, f, k - 1],
                    b2r.at[a, f, k - 1],
                    dev(nxt(z, k), y, c, x),
                )
                for k in range(1, 4)
            ]

        def add(i, _):
            mid[a, f, 2 * i + j] = (
                swap[a, f, i, z].astype(F32) + first[a, f, mate, i].astype(F32)
            ).astype(BF16)
            mid[a, f, 2 * i + jo] = (
                first[a, f, 1, i].astype(F32) + first[a, f, 2 - mate, i].astype(F32)
            ).astype(BF16)
            return 0

        lax.fori_loop(0, 4, add, 0)
        return [
            send(
                mid.at[a, f, pl.ds(2 * nxt(y, k), 2)],
                second.at[a, f, k - 1],
                b2s.at[a, f, k - 1],
                b2r.at[a, f, k - 1],
                dev(z, nxt(y, k), c, x),
            )
            for k in range(1, 4)
        ]

    def return3(a, f, cps):
        recv(cps)
        if zfirst(f):
            fin[j] = mid[a, f, z].astype(F32) + second[a, f, mate, 0].astype(F32)
            fin[jo] = second[a, f, 1, 0].astype(F32) + second[a, f, 2 - mate, 0].astype(F32)
        else:
            fin[...] = (
                mid[a, f, pl.ds(2 * y, 2)].astype(F32)
                + second[a, f, 0].astype(F32)
                + second[a, f, 1].astype(F32)
                + second[a, f, 2].astype(F32)
            )
        return fin[...].reshape(2 * MOST, F)

    def to_x(a, f, rows):
        slots[a, f, x] = rows.reshape(2, MOST, F).astype(BF16)
        return [
            send(
                slots.at[a, f, x],
                slots.at[a, f, x],
                xs.at[a, f, k - 1],
                xr.at[a, f, k - 1],
                (me, nxt(x, k)),
            )
            for k in range(1, 4)
        ]

    def spread(row, stage, cc, n):
        for i in range(D // TILE):
            vsrc[stage, cc, n, i : i + 1, :] = row[:, i * TILE : i * TILE + TILE]

    def vsum1(s, n):
        cut = pl.ds(0, n)
        cps = []
        for i in range(1, 8):
            k, cc = i // 2, (c if i % 2 == 0 else oc)
            cps.append(
                send(
                    vsrc.at[s, cc, cut],
                    vy.at[2 * y + c, cut],
                    vs.at[0, i - 1],
                    vr.at[0, i - 1],
                    dev(z, nxt(y, k), cc, x),
                )
            )
        vy[2 * y + c, cut] = vsrc[s, c, cut]
        return cps

    def vsum2(s, n, cps):
        recv(cps)
        cut = pl.ds(0, n)
        if s == 0:
            total = vy[0, cut]
            for i in range(1, 8):
                total = total + vy[i, cut]
        else:
            total = ((vw[0] + vw[1]) + (vw[2] + vw[3]))[None]
        at = z if s == 0 else x
        vz[s, at, c, cut] = total
        cps = []
        for i in range(1, 8):
            k, cc = i // 2, (c if i % 2 == 0 else oc)
            cps.append(
                send(
                    vz.at[s, at, c, cut],
                    vz.at[s, at, c, cut],
                    vs.at[1 + s, i - 1],
                    vr.at[1 + s, i - 1],
                    dev(nxt(z, k), y, cc, x) if s == 0 else dev(z, y, cc, nxt(x, k)),
                )
            )
        return cps

    def vsum3(s, cps, where):
        recv(cps)
        for cc, n, out in where:
            vec_ref[out] = (vz[s, 0, cc, n] + vz[s, 1, cc, n]) + (vz[s, 2, cc, n] + vz[s, 3, cc, n])

    def xsum1():
        cps = []
        for i in range(1, 8):
            k, cc = i // 2, (c if i % 2 == 0 else oc)
            cps.append(
                send(
                    vsrc.at[1, cc, 0],
                    vx.at[2 * y + c],
                    ws.at[i - 1],
                    wr.at[i - 1],
                    dev(z, nxt(y, k), cc, x),
                )
            )
        vx[2 * y + c] = vsrc[1, c, 0]
        return cps

    def xsum2(cps):
        recv(cps)
        total = vx[0]
        for i in range(1, 8):
            total = total + vx[i]
        vw[z] = total
        return [
            send(vw.at[z], vw.at[z], ws.at[6 + k], wr.at[6 + k], dev(nxt(z, k), y, c, x))
            for k in range(1, 4)
        ]

    drained = [0]

    def drain():
        for cp in pending[drained[0] :]:
            cp.wait_send()
        drained[0] = len(pending)

    parts = range(NF)
    pairs = [(f, f + 1) for f in range(0, NF, 2)]
    last = len(pairs) - 1
    g1, g2, g3 = {}, {}, {}
    r0, r1, r2, r3 = {}, {}, {}, {}

    def each(step, a, p, into, *before):
        for f in pairs[p]:
            into[a, f] = step(a, f, *[b[a, f] for b in before])

    for p in range(last + 1):
        each(gather1, 0, p, g1)
    in_og.wait()
    mixv = dot(table, og[...], 1, 0) * gate_ref[...]
    mix[...] = mixv
    gradv = weight * mixv
    for f in range(NF):
        for jj in range(2):
            own[1, f, jj] = gradv[MOST * jj : MOST * jj + MOST, f * F : f * F + F].astype(BF16)
    in_up = local(up_hbm.at[0], up, loc.at[2])
    in_down = local(down_hbm.at[0], down, loc.at[3])
    each(gather1, 1, 0, g1)
    for p in range(last + 1):
        each(gather2, 0, p, g2, g1)
    for p in range(1, last + 1):
        each(gather1, 1, p, g1)

    recv(tabc)
    tabt = tables[...].astype(F32).reshape(64, TOK).T.astype(BF16)
    table_ref[...] = tabt
    invs = []

    def slot_rows(q):
        sl = slice(16 * q, 16 * q + 16)
        t16 = dot(tables[q], tok[...], 1, 0)
        c16 = t16 - jnp.mean(t16, axis=1, keepdims=True)
        i16 = lax.rsqrt(jnp.mean(c16 * c16, axis=1, keepdims=True) + 1e-06)
        invs.append(i16)
        n64[sl, :] = c16 * i16
        og64[sl, :] = dot(tables[q], og[...], 1, 0).astype(BF16)

    slot_rows(0)
    each(gather2, 1, 0, g2, g1)
    for q in range(1, 4):
        slot_rows(q)
    for p in range(last + 1):
        each(gather3, 0, p, g3, g2)
        if p > 0:
            each(gather2, 1, p, g2, g1)
        else:
            in_up.wait()
        for f in pairs[p]:
            rows_ready(0, f, g3[0, f])
            acc = dot(rowmat0[:, f * F : f * F + F], up[f * F : f * F + F, :], 1, 0)
            pre[...] = acc if f == 0 else pre[...] + acc
    prev = pre[...]
    tang = jnp.tanh(GELU_C * (prev + 0.044715 * prev * prev * prev))
    act[...] = (0.5 * prev * (1.0 + tang)).astype(BF16)
    pre[...] = 0.5 * (1.0 + tang) + 0.5 * prev * (1.0 - tang * tang) * GELU_C * (
        1.0 + 3.0 * 0.044715 * prev * prev
    )
    in_down.wait()
    for p in range(last + 1):
        each(partial, 0, p, r0)
    each(gather3, 1, 0, g3, g2)
    for p in range(last + 1):
        each(return1, 0, p, r1, r0)
    for p in range(last + 1):
        if p > 0:
            each(gather3, 1, p, g3, g2)
        for f in pairs[p]:
            rows_ready(1, f, g3[1, f])
            acc = dot(rowmat1[:, f * F : f * F + F], down[:, f * F : f * F + F], 1, 1)
            gact[...] = acc if f == 0 else gact[...] + acc
    gpre[...] = (gact[...] * pre[...]).astype(BF16)
    for p in range(last + 1):
        each(partial, 1, p, r0)
    each(return2, 0, 0, r2, r1)
    for p in range(last + 1):
        each(return1, 1, p, r1, r0)
    for p in range(1, last + 1):
        each(return2, 0, p, r2, r1)
    grad_w = jnp.zeros((2 * MOST, 1), F32)
    for p in range(last + 1):
        for f in pairs[p]:
            rows = return3(0, f, r2[0, f])
            grad_w = grad_w + jnp.sum(rows * mix[:, f * F : f * F + F], axis=1, keepdims=True)
            r3[0, f] = to_x(0, f, rows * weight)
        if p < last:
            each(return2, 1, p, r2, r1)
    grad_logit = grad_w * weight * (1.0 - weight)
    hg = hid16[...].astype(F32) * grad_logit
    spread(jnp.sum(hg[:MOST], axis=0, keepdims=True), 0, 0, 1)
    spread(jnp.sum(hg[MOST:], axis=0, keepdims=True), 0, 1, 0)
    vsrc[0, 1, 1] = jnp.zeros((8, TILE), F32)
    each(return2, 1, last, r2, r1)
    drain()
    sums1, sums2 = [], []

    def back_rows(f):
        rows = return3(1, f, r2[1, f])
        add = [
            grad_logit[MOST * jj : MOST * jj + MOST]
            * router_ref[jj : jj + 1, f * F : f * F + F].astype(F32)
            for jj in range(2)
        ]
        rows = rows + jnp.concatenate(add, axis=0)
        sums1.append(jnp.sum(rows, axis=0, keepdims=True))
        sums2.append(jnp.sum(rows * n16[:, f * F : f * F + F], axis=0, keepdims=True))
        return rows

    for p in range(last):
        for f in pairs[p]:
            r3[1, f] = to_x(1, f, back_rows(f))
    ends = [back_rows(f) for f in pairs[last]]
    spread(jnp.concatenate(sums1, axis=1), 1, 0, 0)
    spread(jnp.concatenate(sums2, axis=1), 1, 1, 0)
    wa = xsum1()
    for f, rows in zip(pairs[last], ends):
        r3[1, f] = to_x(1, f, rows)
    sums = []
    for f in parts:
        cols = slice(f * F, f * F + F)
        recv(r3[0, f])
        outrows = slots[0, f].astype(F32).reshape(64, F)
        sums.append(jnp.sum(outrows * og64[:, cols].astype(F32), axis=0, keepdims=True))
        x64[:, cols] = outrows.astype(BF16)
    spread(jnp.concatenate(sums, axis=1), 0, 0, 0)
    va = vsum1(0, 2)
    wb = xsum2(wa)
    vb = vsum2(0, 2, va)
    wc = vsum2(1, 1, wb)
    m1 = jnp.zeros((64, 1), F32)
    m2 = jnp.zeros((64, 1), F32)
    for f in parts:
        cols = slice(f * F, f * F + F)
        recv(r3[1, f])
        gh = slots[1, f].astype(F32).reshape(64, F)
        ghn = gh * n64[:, cols]
        one = 1.0 + scale_ref[:, cols]
        g64[:, cols] = gh * one
        m1 = m1 + jnp.sum(gh * one, axis=1, keepdims=True)
        m2 = m2 + jnp.sum(ghn * one, axis=1, keepdims=True)
    m1 = m1 * (1.0 / D)
    m2 = m2 * (1.0 / D)
    for q in range(4):
        sl = slice(16 * q, 16 * q + 16)
        c64[sl, :] = (invs[q] * (g64[sl, :] - m1[sl] - n64[sl, :] * m2[sl])).astype(BF16)
    vsum3(0, vb, [(0, 0, 2), (0, 1, 3), (1, 0, 4)])
    drain()
    vsum3(1, wc, [(0, 0, 0), (1, 0, 1)])


def finish_kernel(
    rows,
    grads,
    act,
    gp,
    mixrows,
    corr,
    tok,
    og,
    table_ref,
    vec_ref,
    gate_ref,
    up_hbm,
    down_hbm,
    block_hbm,
    tgrad_hbm,
    shift_ref,
    scale_ref,
    ggrad_ref,
    router_ref,
    up,
    down,
    block,
    tgrad,
    act_t,
    sem_out,
):
    steps = D // STEP
    for i in range(D // TILE):
        cols = slice(i * TILE, i * TILE + TILE)
        shift_ref[:, cols] = vec_ref[0, i : i + 1, :]
        scale_ref[:, cols] = vec_ref[1, i : i + 1, :]
        ggrad_ref[:, cols] = vec_ref[2, i : i + 1, :]
        router_ref[0:1, cols] = vec_ref[3, i : i + 1, :]
        router_ref[1:2, cols] = vec_ref[4, i : i + 1, :]
    act_t[...] = act[...].astype(F32).T.astype(BF16)
    stores = []

    def store(src, dst, sem):
        cp = pltpu.make_async_copy(src, dst, sem)
        cp.start()
        stores.append(cp)

    for t in range(steps):
        cols = pl.ds(t * STEP, STEP)
        up[cols, :] = dot(rows[:, cols], gp[...], 0, 0).astype(BF16)
        store(up.at[cols], up_hbm.at[0, cols], sem_out.at[t, 0])
        down[:, cols] = dot(act_t[...], grads[:, cols], 1, 0).astype(BF16)
        store(down.at[:, cols], down_hbm.at[0, :, cols], sem_out.at[t, 1])
        block[:, cols] = (
            tok[:, cols].astype(F32)
            + gate_ref[:, cols] * dot(table_ref[...], mixrows[:, cols], 1, 0)
        ).astype(BF16)
        store(block.at[:, cols], block_hbm.at[:, cols], sem_out.at[t, 2])
        tgrad[:, cols] = (
            og[:, cols].astype(F32) + dot(table_ref[...], corr[:, cols], 1, 0)
        ).astype(BF16)
        store(tgrad.at[:, cols], tgrad_hbm.at[:, cols], sem_out.at[t, 3])
    for cp in stores:
        cp.wait()


def per_device(tokens, shift, scale, gate, router, up, down, picks, out_grad):
    hbm = pl.BlockSpec(memory_space=pl.ANY)
    vmem = pl.BlockSpec(memory_space=pltpu.VMEM)
    dma = pltpu.SemaphoreType.DMA
    shape = jax.ShapeDtypeStruct
    vm = pltpu.VMEM
    *kept, table, vec = pl.pallas_call(
        exchange_kernel,
        out_shape=(
            vm((SLOTS, D), BF16),
            vm((SLOTS, D), BF16),
            vm((SLOTS, HU), BF16),
            vm((SLOTS, HU), BF16),
            vm((64, D), BF16),
            vm((64, D), BF16),
            vm((TOK, D), BF16),
            vm((TOK, D), BF16),
            vm((TOK, 64), BF16),
            vm((5, 8, TILE), F32),
        ),
        in_specs=[hbm, hbm, vmem, vmem, vmem, vmem, hbm, hbm, vmem],
        out_specs=(vmem,) * 10,
        scratch_shapes=[
            pltpu.VMEM((D, HU), BF16),
            pltpu.VMEM((HU, D), BF16),
            pltpu.VMEM((2, NF, 2, MOST, F), BF16),
            pltpu.VMEM((2, NF, 2, 4, 4, MOST, F), BF16),
            pltpu.VMEM((2, NF // 2, 4, 2, MOST, F), BF16),
            pltpu.VMEM((SLOTS, HU), F32),
            pltpu.VMEM((SLOTS, HU), F32),
            pltpu.VMEM((2, NF, 2, 4, 4, MOST, F), BF16),
            pltpu.VMEM((2, NF, 4, 4, MOST, F), BF16),
            pltpu.VMEM((2, NF, 3, 4, MOST, F), BF16),
            pltpu.VMEM((2, NF, 8, MOST, F), BF16),
            pltpu.VMEM((2, NF, 3, 2, MOST, F), BF16),
            pltpu.VMEM((2, MOST, F), F32),
            pltpu.VMEM((2, NF, 4, 2, MOST, F), BF16),
            pltpu.VMEM((4, 2 * MOST, TOK), BF16),
            pltpu.VMEM((2 * MOST, D), F32),
            pltpu.VMEM((2 * MOST, D), BF16),
            pltpu.VMEM((64, D), F32),
            pltpu.VMEM((64, D), BF16),
            pltpu.VMEM((64, D), F32),
            pltpu.VMEM((2 * MOST, D), F32),
            pltpu.VMEM((2, 2, 2, 8, TILE), F32),
            pltpu.VMEM((8, 2, 8, TILE), F32),
            pltpu.VMEM((8, 8, TILE), F32),
            pltpu.VMEM((4, 8, TILE), F32),
            pltpu.VMEM((2, 4, 2, 2, 8, TILE), F32),
            dma((4,)),
            dma((3,)),
            dma((3,)),
            dma((2, NF, 3)),
            dma((2, NF, 3)),
            dma((2, NF, 3)),
            dma((2, NF, 3)),
            dma((2, NF)),
            dma((2, NF)),
            dma((2, NF)),
            dma((2, NF)),
            dma((2, NF, 3)),
            dma((2, NF, 3)),
            dma((2, NF, 3)),
            dma((2, NF, 3)),
            dma((2, NF, 3)),
            dma((2, NF, 3)),
            dma((3, 7)),
            dma((3, 7)),
            dma((10,)),
            dma((10,)),
        ],
        compiler_params=pltpu.CompilerParams(
            collective_id=0, has_side_effects=True, vmem_limit_bytes=55 * 2**20
        ),
        cost_estimate=pl.CostEstimate(
            flops=12 * SLOTS * D * HU, bytes_accessed=24 * 2**20, transcendentals=SLOTS * HU
        ),
    )(
        tokens,
        out_grad,
        shift.reshape(1, D),
        scale.reshape(1, D),
        gate.reshape(1, D),
        router[0].T,
        up,
        down,
        picks[0],
    )
    kept = [pltpu.with_memory_space_constraint(a, vm) for a in (*kept, table, vec)]
    up_grad, down_grad, block, tgrad, shift_g, scale_g, gate_g, router_g = pl.pallas_call(
        finish_kernel,
        out_shape=(
            shape((1, D, HU), BF16),
            shape((1, HU, D), BF16),
            shape((TOK, D), BF16),
            shape((TOK, D), BF16),
            shape((1, D), F32),
            shape((1, D), F32),
            shape((1, D), F32),
            shape((2, D), F32),
        ),
        in_specs=[vmem] * 11,
        out_specs=(hbm, hbm, hbm, hbm, vmem, vmem, vmem, vmem),
        scratch_shapes=[
            vm((D, HU), BF16),
            vm((HU, D), BF16),
            vm((TOK, D), BF16),
            vm((TOK, D), BF16),
            vm((HU, SLOTS), BF16),
            dma((D // STEP, 4)),
        ],
        compiler_params=pltpu.CompilerParams(vmem_limit_bytes=44 * 2**20),
        cost_estimate=pl.CostEstimate(
            flops=4 * SLOTS * D * HU, bytes_accessed=10 * 2**20, transcendentals=0
        ),
    )(*kept, gate.reshape(1, D))
    return (
        block,
        tgrad,
        up_grad,
        down_grad,
        router_g.T[None],
        shift_g[0],
        scale_g[0],
        gate_g[0],
    )


def solution(mesh):
    in_specs = (
        P("ctx", None),
        P(),
        P(),
        P(),
        P("exp", None, None),
        P("exp", None, "ctx"),
        P("exp", "ctx", None),
        P("exp", None, None),
        P("ctx", None),
    )
    out_specs = (
        P("ctx", None),
        P("ctx", None),
        P("exp", None, "ctx"),
        P("exp", "ctx", None),
        P("exp", None, None),
        P(),
        P(),
        P(),
    )
    return jax.shard_map(
        per_device, mesh=mesh, in_specs=in_specs, out_specs=out_specs, check_vma=False
    )
```
